512 devices in a mesh: slab: 128 (over y, z, core), grp: 4 (over x).
Axes of the slice: x: 4, y: 8, z: 8, core: 2. Of those that a mesh axis runs over, the one named last changes fastest.
Arguments:
- potential: bfloat16 [1024, 8, 1024], P('slab'), may hold values from -3 to 3
- coefficients: bfloat16 [2048, 16, 8, 1024], P(('slab', 'grp')), may hold values from -1 to 1
- box_center: int32 [2048], replicated, may hold values from 0 to 1023, as said below
- box_extent: int32 [2048], replicated, may hold values from 8 to 16
Outputs:
- margin: float32 [2048, 80], P(('slab', 'grp'))
- hamiltonian: float32 [2048, 80], P(('slab', 'grp'))
The draws below stay inside these ranges and needn't reach their ends.
Inputs may be any that keep to these rules, and one draw needn't show every extreme that they name: `box_center`: function b's centre lies among the 8 planes of slab b // 16, that is from (8 * (b // 16)) on.
All inputs are finite; a program needn't handle non-finite values.
Results may differ from the reference program's by a relative error of at most 0.0003.
Values may be sent and summed in bfloat16 or wider, within the bound.
No kernel may reach another device: no remote copies, remote signals or barrier semaphores. Data moves between devices by JAX's collectives and lax.ppermute only.
A program may use at most 64 MiB of HBM per device.

```python
import jax
import jax.numpy as jnp
from jax import lax

SZ = 8
EMAX = 16
COMP = 8
CX = 32
CY = 32
HW = 8
CS = 1024
NZ = 1024
MEMBERS = 16
FUNCS = 2048
BAND = 80
N_SLAB = 128


def draw_coefficients(key, part):
    keys = jax.random.split(jax.random.fold_in(key, 17), 3)
    centre_x = jax.random.uniform(keys[0], (FUNCS, 1), minval=0.0, maxval=float(CX))
    centre_y = jax.random.uniform(keys[1], (FUNCS, 1), minval=0.0, maxval=float(CY))
    cells = jnp.arange(CX * CY)
    cell_x = (cells // CY).astype(jnp.float32)[None, :]
    cell_y = (cells % CY).astype(jnp.float32)[None, :]
    delta_x = cell_x - centre_x
    delta_y = cell_y - centre_y
    envelope = 0.05 + jnp.exp(-(delta_x * delta_x + delta_y * delta_y) / 4.5)
    energy = jnp.sum(envelope * envelope, axis=1, keepdims=True)
    amplitude = 1.0 / jnp.sqrt(energy * float(EMAX * COMP))
    shape = (FUNCS, EMAX, COMP, CX * CY)
    base = jax.random.truncated_normal(keys[2], -6.0, 6.0, shape)
    values = base * (amplitude * envelope)[:, None, None, :]
    return values.astype(jnp.bfloat16)


def draw_box_center(key, part):
    offsets = jax.random.randint(jax.random.fold_in(key, 29), (FUNCS,), 0, SZ)
    owner = jnp.arange(FUNCS, dtype=jnp.int32) // (FUNCS // N_SLAB)
    return (owner * SZ + offsets).astype(jnp.int32)


def plant(array, own_key, low, largest):
    index_at = [jax.random.randint(jax.random.fold_in(own_key, axis), (), 0, length) for axis, length in enumerate(array.shape)]
    widest = array.shape.index(max(array.shape))
    next_to = index_at[:widest] + [(index_at[widest] + 1) % array.shape[widest]] + index_at[widest + 1:]
    return array.at[tuple(index_at)].set(low).at[tuple(next_to)].set(largest)


def levels(stream_key, dims, cuts, smallest, largest):
    def one(axis_at, blocks):
        draws = jax.random.uniform(jax.random.fold_in(jax.random.fold_in(stream_key, 6), axis_at), (blocks,), jnp.float32, smallest / len(cuts), largest / len(cuts))
        return jnp.repeat(jnp.exp(draws), dims[axis_at] // blocks).reshape((-1,) + (1,) * (len(dims) - axis_at - 1))

    loudness = one(*cuts[0])
    for cut in cuts[1:]:
        loudness = loudness * one(*cut)
    return loudness


def setup_inputs(seed: int = 0) -> dict:
    key_of = jax.random.split(jax.random.key(seed), 5)
    return {
        "potential": jnp.clip(jax.random.uniform(key_of[0], (NZ, COMP, CS), jnp.float32, -3.0, 3.0) * levels(key_of[0], (NZ, COMP, CS), ((0, 128),), -0.4, 0.0), -3.0, 3.0).astype(jnp.bfloat16),
        "coefficients": draw_coefficients(jax.random.fold_in(key_of[4], 71), 0),
        "box_center": draw_box_center(jax.random.fold_in(key_of[4], 71), 0),
        "box_extent": plant(jax.random.randint(key_of[3], (FUNCS,), EMAX // 2, EMAX + 1), jax.random.fold_in(key_of[3], 1), EMAX // 2, EMAX).astype(jnp.int32),
    }


def haar_signs():
    row_ids = jnp.arange(COMP, dtype=jnp.int32)[:, None]
    col_ids = jnp.arange(COMP, dtype=jnp.int32)[None, :]
    common = jnp.bitwise_and(row_ids, col_ids)
    parity = (common % 2 + (common // 2) % 2 + (common // 4) % 2) % 2
    return (1 - 2 * parity).astype(jnp.float32)


def apply_hamiltonian(orbital, pot_box, inside):
    shaped = orbital.reshape(orbital.shape[:3] + (CX, CY))
    bordered = jnp.pad(shaped, ((0, 0), (0, 0), (0, 0), (1, 1), (1, 1)))
    beside_all = bordered[:, :, :, 2:, 1:-1] + bordered[:, :, :, :-2, 1:-1] + bordered[:, :, :, 1:-1, 2:] + bordered[:, :, :, 1:-1, :-2]
    plane_term = (2.0 * shaped - 0.5 * beside_all).reshape(orbital.shape)
    padded = jnp.pad(orbital, ((0, 0), (1, 1), (0, 0), (0, 0)))
    depth_term = orbital - 0.5 * (padded[:, :-2] + padded[:, 2:])
    haar_table = haar_signs()
    fine_values = jnp.einsum("kc,npcx->npkx", haar_table, orbital, precision=lax.Precision.HIGHEST)
    potential_term = jnp.einsum("kc,npkx->npcx", haar_table, pot_box * fine_values, precision=lax.Precision.HIGHEST) / COMP
    return jnp.where(inside, plane_term + depth_term + potential_term, 0.0).astype(jnp.bfloat16)


def place_planes(starts, frame_depth, tile_data):
    source = jnp.arange(EMAX, dtype=jnp.int32)
    target = jnp.arange(frame_depth, dtype=jnp.int32)
    onehot = (starts[:, None, None] + source[None, None, :] == target[None, :, None]).astype(jnp.float32)
    return jnp.einsum("nqp,npcx->nqcx", onehot, tile_data, precision=lax.Precision.HIGHEST)


def reference(potential, coefficients, box_center, box_extent):
    frame_depth = SZ + EMAX
    planes = jnp.arange(EMAX, dtype=jnp.int32)
    member_ids = jnp.arange(MEMBERS, dtype=jnp.int32)
    steps_away = jnp.arange(5, dtype=jnp.int32) - 2

    def per_slab(slab_index):
        band_slabs = (slab_index + steps_away) % N_SLAB
        band_rows = (band_slabs[:, None] * MEMBERS + member_ids[None, :]).reshape(-1)
        centers = jnp.take(box_center, band_rows)
        extents = jnp.take(box_extent, band_rows)
        shifts = jnp.repeat(steps_away, MEMBERS, total_repeat_length=BAND)
        home = jnp.repeat(band_slabs, MEMBERS, total_repeat_length=BAND)
        relative = centers - home * SZ + shifts * SZ - extents // 2 + HW
        inside = planes[None, :] < extents[:, None]
        values = jnp.take(coefficients, band_rows, axis=0).astype(jnp.float32)
        orbital = jnp.where(inside[:, :, None, None], values, 0.0)
        window = place_planes(relative, frame_depth, orbital)
        own_orbital = orbital[2 * MEMBERS:3 * MEMBERS]
        own_relative = relative[2 * MEMBERS:3 * MEMBERS]
        own_inside = inside[2 * MEMBERS:3 * MEMBERS]
        plane_ids = (slab_index * SZ + own_relative - HW)[:, None] + planes[None, :]
        pot_box = jnp.take(potential, plane_ids % NZ, axis=0).astype(jnp.float32)
        applied = apply_hamiltonian(own_orbital, pot_box, own_inside[:, :, None, None])
        applied_window = place_planes(own_relative, frame_depth, applied.astype(jnp.float32))
        flat_window = window.reshape(window.shape[0], -1)
        own_window = window[2 * MEMBERS:3 * MEMBERS].reshape(MEMBERS, -1)
        margin_rows = jnp.dot(own_window, flat_window.T, precision=lax.Precision.HIGHEST)
        ham_rows = jnp.dot(applied_window.reshape(MEMBERS, -1), flat_window.T, precision=lax.Precision.HIGHEST)
        return margin_rows, ham_rows

    margin, hamiltonian = lax.map(per_slab, jnp.arange(N_SLAB, dtype=jnp.int32))
    return margin.reshape(FUNCS, BAND), hamiltonian.reshape(FUNCS, BAND)
```

```python
import jax
import jax.numpy as jnp
from jax import lax
from jax.experimental import pallas as pl
from jax.experimental.pallas import tpu as pltpu
from jax.sharding import PartitionSpec as P

GROUPS = 4
PER = 4
MEMBERS = 16
DEPTH = 16
SZ = 8
COMP = 8
CY = 32
SEG = 256
LANES = 128
PLANE = COMP * SEG
MAIN = SZ * PLANE
EDGE = MAIN + PLANE
FULL = MAIN + 2 * PLANE
HALO = SZ * COMP * CY
STRIDE = 27 * COMP
VMEM = 40 * 1024 * 1024
F32 = jnp.float32
BF16 = jnp.bfloat16


def params():
    return pltpu.CompilerParams(vmem_limit_bytes=VMEM)


def pack_kernel(main_ref, next_ref, out_ref):
    lane = lax.broadcasted_iota(jnp.int32, (32, LANES), 1)
    for f in range(PER):
        out_ref[0, f, 0:128, :] = main_ref[f, :, 0:LANES]
        out_ref[0, f, 128:256, :] = main_ref[f, :, LANES:SEG]
        after = next_ref[f].astype(F32)
        packed = after[0:32]
        for i in range(1, 4):
            moved = pltpu.roll(after[32 * i : 32 * i + 32], 32 * i, 1)
            packed = jnp.where(lane < 32 * i, packed, moved)
        out_ref[0, f, 256:288, :] = packed.astype(BF16)


def pack(coefficients):
    rows = coefficients.reshape(PER, DEPTH * COMP, GROUPS * SEG)
    return pl.pallas_call(
        pack_kernel,
        grid=(GROUPS,),
        in_specs=[
            pl.BlockSpec((PER, DEPTH * COMP, SEG), lambda d: (0, 0, d)),
            pl.BlockSpec((PER, DEPTH * COMP, LANES), lambda d: (0, 0, jnp.minimum(2 * d + 2, 7))),
        ],
        out_specs=pl.BlockSpec((1, PER, 288, LANES), lambda d: (d, 0, 0, 0)),
        out_shape=jax.ShapeDtypeStruct((GROUPS, PER, 288, LANES), BF16),
        compiler_params=params(),
    )(rows, rows)


def place_kernel(start_ref, extent_ref, in_ref, low_ref, mid_ref, up_ref, s0, s1, sh):
    zero = jnp.zeros((STRIDE, LANES), F32)
    row = lax.broadcasted_iota(jnp.int32, (128, LANES), 0)
    lane16 = lax.broadcasted_iota(jnp.int32, (16, LANES), 1)

    def spread(n, carry):
        base = pl.multiple_of(n * STRIDE, 8)
        for s in (s0, s1, sh):
            s[pl.ds(base, STRIDE), :] = zero
        at = pl.multiple_of(base + start_ref[n] * COMP, 8)
        inside = row < extent_ref[n] * COMP
        s0[pl.ds(at, 128), :] = jnp.where(inside, in_ref[n, 0:128, :].astype(F32), 0.0)
        s1[pl.ds(at, 128), :] = jnp.where(inside, in_ref[n, 128:256, :].astype(F32), 0.0)
        packed = in_ref[n, 256:288, :].astype(F32)
        for i in range(4):
            part = packed if i == 0 else pltpu.roll(packed, LANES - 32 * i, 1)
            part = jnp.where(inside[32 * i : 32 * i + 32], part, 0.0)
            sh[pl.ds(pl.multiple_of(at + 32 * i, 8), 32), :] = part
        return carry

    lax.fori_loop(0, MEMBERS, spread, 0)

    def rows_of(s, r):
        a = s[pl.ds(r, 8, stride=STRIDE), :]
        b = s[pl.ds(8 * STRIDE + r, 8, stride=STRIDE), :]
        return jnp.concatenate([a, b], axis=0)

    for f in range(25):
        for c in range(COMP):
            for h, s in ((0, s0), (1, s1)):
                tile = rows_of(s, f * COMP + c).astype(BF16)
                for ref, first, count in ((low_ref, 0, 9), (mid_ref, 7, 10), (up_ref, 15, 9)):
                    q = f - first
                    if 0 <= q < count:
                        at = (q * COMP + c) * SEG + h * LANES
                        ref[:, at : at + LANES] = tile
    for ref, first, base in ((low_ref, 0, EDGE), (mid_ref, 8, FULL), (up_ref, 16, EDGE)):
        for j in range(2):
            for c in range(COMP):
                packed = rows_of(sh, (first + 4 * j) * COMP + c)
                for i in range(1, 4):
                    moved = pltpu.roll(rows_of(sh, (first + 4 * j + i) * COMP + c), 32 * i, 1)
                    packed = jnp.where(lane16 < 32 * i, packed, moved)
                at = base + (j * COMP + c) * LANES
                ref[:, at : at + LANES] = packed.astype(BF16)


def place(starts, extents, got):
    scratch = pltpu.VMEM((MEMBERS * STRIDE, LANES), F32)
    whole = pl.BlockSpec(memory_space=pltpu.VMEM)
    scalars = pl.BlockSpec(memory_space=pltpu.SMEM)
    return pl.pallas_call(
        place_kernel,
        in_specs=[scalars, scalars, whole],
        out_specs=[whole] * 3,
        out_shape=[
            jax.ShapeDtypeStruct((MEMBERS, EDGE + HALO), BF16),
            jax.ShapeDtypeStruct((MEMBERS, FULL + HALO), BF16),
            jax.ShapeDtypeStruct((MEMBERS, EDGE + HALO), BF16),
        ],
        scratch_shapes=[scratch] * 3,
        compiler_params=params(),
    )(starts, extents, got.reshape(MEMBERS, 288, LANES))


def signed_sums(values):
    values = list(values)
    for bit in (1, 2, 4):
        values = [
            values[k ^ bit] - values[k] if k & bit else values[k] + values[k ^ bit]
            for k in range(COMP)
        ]
    return values


def apply_planes(src, dst, row_at, dst_at, dst_lane, where_ref, pot_ref, lap_ref):
    rel = where_ref[pl.ds(row_at, 16), 0:1]
    ext = where_ref[pl.ds(row_at, 16), 1:2]

    def one(q, carry):
        def plane(at, c):
            lanes = pl.multiple_of(at * PLANE + c * SEG, LANES)
            return src[pl.ds(row_at, 16), pl.ds(lanes, SEG)]

        here = [plane(q + 1, c) for c in range(COMP)]
        plane_term = jnp.dot(
            jnp.concatenate(here, axis=0), lap_ref[...], preferred_element_type=F32
        )
        inside = jnp.where((q >= rel) & (q < rel + ext), -0.5, 0.0)
        orbital = [v.astype(F32) for v in here]
        fine = signed_sums(orbital)
        pot = pot_ref[pl.ds(pl.multiple_of(q * COMP, 8), COMP), :]
        back = signed_sums([fine[k] * pot[k : k + 1] for k in range(COMP)])
        for c in range(COMP):
            beside = plane(q, c).astype(F32) + plane(q + 2, c).astype(F32)
            total = plane_term[16 * c : 16 * c + 16] + back[c]
            total += orbital[c] + inside * beside
            lanes = pl.multiple_of(dst_lane + q * PLANE + c * SEG, LANES)
            dst[pl.ds(dst_at, 16), pl.ds(lanes, SEG)] = total.astype(BF16)
        return carry

    lax.fori_loop(0, SZ, one, 0)


def middle_kernel(mid_ref, where_ref, pot_ref, lap_ref, out_ref):
    apply_planes(mid_ref, out_ref, 0, 0, 0, where_ref, pot_ref, lap_ref)


def middle(mid, where, pot, laplace):
    return pl.pallas_call(
        middle_kernel,
        out_shape=jax.ShapeDtypeStruct((MEMBERS, MAIN), BF16),
        compiler_params=params(),
        cost_estimate=pl.CostEstimate(flops=40_000_000, bytes_accessed=6_000_000, transcendentals=0),
    )(mid, where, pot, laplace)


CONTRACT = (((1,), (1,)), ((), ()))


def gram_kernel(
    share_ref, lower_ref, mid_ref, upper_ref, done_ref, where_ref, pot_ref, lap_ref, out_ref, both, last, halo, sums
):
    blank = jnp.zeros((16, PLANE), BF16)
    both[0:16, 0:EDGE] = lower_ref[:, 0:EDGE]
    both[0:16, EDGE:FULL] = blank
    both[16:32, :] = mid_ref[:, 0:FULL]
    both[32:48, 0:PLANE] = blank
    both[32:48, PLANE:FULL] = upper_ref[:, 0:EDGE]
    both[64:80, PLANE:EDGE] = done_ref[...]
    halo[0:16, :] = lower_ref[:, EDGE : EDGE + HALO]
    halo[16:32, :] = mid_ref[:, FULL : FULL + HALO]
    halo[32:48, :] = upper_ref[:, EDGE : EDGE + HALO]
    for at in (0, 32):
        apply_planes(both, both, at, 48 + at, PLANE, where_ref, pot_ref, lap_ref)
    lane = lax.broadcasted_iota(jnp.int32, (48, LANES), 1)
    for j in range(2):
        for c in range(COMP):
            packed = None
            for i in range(4):
                at = PLANE + ((4 * j + i) * COMP + c) * SEG + LANES
                piece = both[0:48, at : at + LANES].astype(F32)
                if i < 3:
                    piece = pltpu.roll(piece, 32 * (i + 1), 1)
                packed = piece if packed is None else jnp.where(lane < 32 * i, packed, piece)
            at = (j * COMP + c) * LANES
            last[:, at : at + LANES] = packed.astype(BF16)

    def step(q, total):
        lanes = pl.ds(pl.multiple_of(PLANE + q * PLANE, LANES), PLANE)
        return total + lax.dot_general(
            both[:, lanes], both[0:48, lanes], CONTRACT, preferred_element_type=F32
        )

    main = lax.fori_loop(0, SZ, step, jnp.zeros((96, 48), F32))
    cross = lax.dot_general(last[...], halo[...], CONTRACT, preferred_element_type=F32)
    cross += lax.dot_general(halo[...], last[...], CONTRACT, preferred_element_type=F32)
    sums[...] = jnp.zeros((96, LANES), F32)
    sums[0:48, 0:48] = main[0:48]
    sums[48:96, 0:48] = main[48:96] + jnp.where(share_ref[0] > 0, -0.5, 0.0) * cross
    sums[0:48, :] = sums[0:48, :] + pltpu.roll(sums[48:96, :], 64, 1)
    for d in range(GROUPS):
        for k in range(3):
            out_ref[d, PER * k : PER * k + PER, :] = sums[16 * k + PER * d : 16 * k + PER * d + PER, :]


def gram(share, lower, mid, upper, done, where, pot, laplace):
    whole = pl.BlockSpec(memory_space=pltpu.VMEM)
    return pl.pallas_call(
        gram_kernel,
        in_specs=[pl.BlockSpec(memory_space=pltpu.SMEM)] + [whole] * 7,
        out_specs=whole,
        out_shape=jax.ShapeDtypeStruct((GROUPS, 3 * PER, LANES), F32),
        scratch_shapes=[
            pltpu.VMEM((96, FULL), BF16),
            pltpu.VMEM((48, HALO), BF16),
            pltpu.VMEM((48, HALO), BF16),
            pltpu.VMEM((96, LANES), F32),
        ],
        compiler_params=params(),
    )(share, lower, mid, upper, done, where, pot, laplace)


def segment_laplace():
    cells = jnp.arange(SEG, dtype=jnp.int32)
    x, y = cells // CY, cells % CY
    step_x = jnp.abs(x[:, None] - x[None, :])
    step_y = jnp.abs(y[:, None] - y[None, :])
    return jnp.where(
        step_x + step_y == 0, 2.0, jnp.where(step_x + step_y == 1, -0.5, 0.0)
    ).astype(BF16)


def shifted(value, axis, steps):
    count = lax.axis_size(axis)
    return lax.ppermute(value, axis, [(i, (i + steps) % count) for i in range(count)])


def local(potential, coefficients, box_center, box_extent):
    slab = lax.axis_index("slab")
    group = lax.axis_index("grp")
    slabs = lax.axis_size("slab")

    def frames(step):
        source = (slab + step) % slabs
        extents = lax.dynamic_slice_in_dim(box_extent, source * MEMBERS, MEMBERS)
        centers = lax.dynamic_slice_in_dim(box_center, source * MEMBERS, MEMBERS)
        return centers - source * SZ - extents // 2 + step * SZ, extents

    around = [frames(step) for step in (-1, 0, 1)]
    where = jnp.stack(
        [jnp.concatenate([r for r, _ in around]), jnp.concatenate([e for _, e in around])], axis=1
    )
    starts, extents = around[1]
    pot = lax.dynamic_slice_in_dim(potential, group * SEG, SEG, axis=2)
    pot = pot.reshape(SZ * COMP, SEG).astype(F32) * (1.0 / COMP)
    laplace = segment_laplace()
    share = (group < GROUPS - 1).astype(jnp.int32).reshape(1)

    got = lax.all_to_all(pack(coefficients), "grp", 0, 0, tiled=True)
    low, mid, up = place(starts + SZ, extents, got)
    lower = shifted(up, "slab", 1)
    upper = shifted(low, "slab", -1)
    done = middle(mid, where[MEMBERS : 2 * MEMBERS], pot, laplace)
    parts = gram(share, lower, mid, upper, done, where, pot, laplace)
    rows = jnp.sum(lax.all_to_all(parts, "grp", 0, 0, tiled=True), axis=0)
    from_above = shifted(rows[0:PER], "slab", -1)
    own = rows[PER : 2 * PER]
    from_below = shifted(rows[2 * PER :], "slab", 1)

    def band(first):
        out = 0.0
        for block, at in ((from_below, 0), (own, 16), (from_above, 32)):
            out += jnp.pad(block[:, first : first + 48], ((0, 0), (at, 32 - at)))
        return out

    return band(0), band(64)


def solution(mesh):
    return jax.shard_map(
        local,
        mesh=mesh,
        in_specs=(P("slab", None, None), P(("slab", "grp"), None, None, None), P(), P()),
        out_specs=(P(("slab", "grp"), None), P(("slab", "grp"), None)),
        check_vma=False,
    )
```

```python
import jax
import jax.numpy as jnp
from jax import lax
from jax.experimental import pallas as pl
from jax.experimental.pallas import tpu as pltpu
from jax.sharding import PartitionSpec as P

GROUPS = 4
PER = 4
MEMBERS = 16
DEPTH = 16
SZ = 8
COMP = 8
CY = 32
SEG = 256
LANES = 128
PLANE = COMP * SEG
MAIN = SZ * PLANE
EDGE = MAIN + PLANE
FULL = MAIN + 2 * PLANE
HALO = SZ * COMP * CY
STRIDE = 27 * COMP
VMEM = 20 * 1024 * 1024
F32 = jnp.float32
BF16 = jnp.bfloat16


SMALL = pl.CostEstimate(flops=1, bytes_accessed=1, transcendentals=0)


def params():
    return pltpu.CompilerParams(vmem_limit_bytes=VMEM)


def pack_kernel(in_ref, out_ref, tiles, after, sems):
    nexts = [
        pltpu.make_async_copy(in_ref.at[:, :, pl.ds((d + 1) * SEG, LANES)], after.at[d], sems.at[d])
        for d in range(GROUPS - 1)
    ]
    mains = [
        [
            pltpu.make_async_copy(
                in_ref.at[:, :, pl.ds(d * SEG + h * LANES, LANES)],
                tiles.at[d, :, pl.ds(h * 128, 128), :],
                sems.at[3 + 2 * d + h],
            )
            for h in range(2)
        ]
        for d in range(GROUPS)
    ]
    outs = [pltpu.make_async_copy(tiles.at[d], out_ref.at[d], sems.at[11 + d]) for d in range(GROUPS)]
    for d in range(GROUPS):
        if d < GROUPS - 1:
            nexts[d].start()
        for copy in mains[d]:
            copy.start()
    lane = lax.broadcasted_iota(jnp.int32, (32, LANES), 1)
    for d in range(GROUPS):
        if d < GROUPS - 1:
            nexts[d].wait()
            for f in range(PER):
                rows = after[d, f].astype(F32)
                tile = rows[0:32]
                for i in range(1, 4):
                    moved = pltpu.roll(rows[32 * i : 32 * i + 32], 32 * i, 1)
                    tile = jnp.where(lane < 32 * i, tile, moved)
                tiles[d, f, 256:288, :] = tile.astype(BF16)
        else:
            tiles[d, :, 256:288, :] = jnp.zeros((PER, 32, LANES), BF16)
        for copy in mains[d]:
            copy.wait()
        outs[d].start()
    for copy in outs:
        copy.wait()


def pack(coefficients):
    rows = coefficients.reshape(PER, DEPTH * COMP, GROUPS * SEG)
    return pl.pallas_call(
        pack_kernel,
        in_specs=[pl.BlockSpec(memory_space=pl.ANY)],
        out_specs=pl.BlockSpec(memory_space=pl.ANY),
        out_shape=jax.ShapeDtypeStruct((GROUPS, PER, 288, LANES), BF16),
        scratch_shapes=[
            pltpu.VMEM((GROUPS, PER, 288, LANES), BF16),
            pltpu.VMEM((GROUPS - 1, PER, DEPTH * COMP, LANES), BF16),
            pltpu.SemaphoreType.DMA((15,)),
        ],
        compiler_params=pltpu.CompilerParams(vmem_limit_bytes=60 * 1024 * 1024),
    )(rows)


def rows_of(frames, r):
    a = frames[pl.ds(r, 8, stride=STRIDE), :]
    b = frames[pl.ds(8 * STRIDE + r, 8, stride=STRIDE), :]
    return jnp.concatenate([a, b], axis=0)


def gather(ref, frames, first, planes, halo_first, base):
    s0, s1, sh = frames
    lane = lax.broadcasted_iota(jnp.int32, (MEMBERS, LANES), 1)
    for r in range(planes * COMP):
        for h, s in ((0, s0), (1, s1)):
            ref[:, r * SEG + h * LANES : r * SEG + h * LANES + LANES] = rows_of(s, first + r).astype(BF16)
    for j in range(2):
        for c in range(COMP):
            packed = rows_of(sh, halo_first + 4 * j * COMP + c)
            for i in range(1, 4):
                moved = pltpu.roll(rows_of(sh, halo_first + (4 * j + i) * COMP + c), 32 * i, 1)
                packed = jnp.where(lane < 32 * i, packed, moved)
            at = base + (j * COMP + c) * LANES
            ref[:, at : at + LANES] = packed.astype(BF16)


def place_kernel(odd_ref, start_ref, extent_ref, in_ref, across_ref, s0, s1, sh):
    zero = jnp.zeros((11 * COMP, LANES), F32)
    row = lax.broadcasted_iota(jnp.int32, (128, LANES), 0)

    for n in range(MEMBERS):
        base = n * STRIDE
        for s in (s0, s1, sh):
            s[base : base + 11 * COMP, :] = zero
            s[base + 16 * COMP : base + 27 * COMP, :] = zero
        at = pl.multiple_of(base + start_ref[n] * COMP, 8)
        inside = row < extent_ref[n] * COMP
        s0[pl.ds(at, 128), :] = jnp.where(inside, in_ref[n, 0:128, :].astype(F32), 0.0)
        s1[pl.ds(at, 128), :] = jnp.where(inside, in_ref[n, 128:256, :].astype(F32), 0.0)
        packed = in_ref[n, 256:288, :].astype(F32)
        for i in range(4):
            part = packed if i == 0 else pltpu.roll(packed, LANES - 32 * i, 1)
            part = jnp.where(inside[32 * i : 32 * i + 32], part, 0.0)
            sh[pl.ds(pl.multiple_of(at + 32 * i, 8), 32), :] = part
    odd = odd_ref[0]
    gather(across_ref, (s0, s1, sh), odd * (15 * COMP), 9, odd * (16 * COMP), EDGE)


def place(odd, starts, extents, got):
    whole = pl.BlockSpec(memory_space=pltpu.VMEM)
    scalars = pl.BlockSpec(memory_space=pltpu.SMEM)
    return pl.pallas_call(
        place_kernel,
        in_specs=[scalars] * 3 + [whole],
        out_specs=[whole] * 4,
        out_shape=[jax.ShapeDtypeStruct((MEMBERS, EDGE + HALO), BF16)]
        + [jax.ShapeDtypeStruct((MEMBERS * STRIDE, LANES), F32)] * 3,
        compiler_params=params(),
    )(odd, starts, extents, got.reshape(MEMBERS, 288, LANES))


def place_near_kernel(odd_ref, _across, s0, s1, sh, chip_ref, mid_ref):
    even = 1 - odd_ref[0]
    gather(chip_ref, (s0, s1, sh), even * (15 * COMP), 9, even * (16 * COMP), EDGE)
    gather(mid_ref, (s0, s1, sh), 7 * COMP, 10, 8 * COMP, FULL)


def place_near(odd, across, frames):
    whole = pl.BlockSpec(memory_space=pltpu.VMEM)
    return pl.pallas_call(
        place_near_kernel,
        in_specs=[pl.BlockSpec(memory_space=pltpu.SMEM), pl.BlockSpec(memory_space=pl.ANY)] + [whole] * 3,
        out_specs=[whole] * 2,
        out_shape=[
            jax.ShapeDtypeStruct((MEMBERS, EDGE + HALO), BF16),
            jax.ShapeDtypeStruct((MEMBERS, FULL + HALO), BF16),
        ],
        compiler_params=params(),
        cost_estimate=SMALL,
    )(odd, across, *frames)


def signed_sums(values):
    values = list(values)
    for bit in (1, 2, 4):
        values = [
            values[k ^ bit] - values[k] if k & bit else values[k] + values[k ^ bit]
            for k in range(COMP)
        ]
    return values


def apply_planes(src, src_at, dst, dst_at, where_ref, where_at, pot_ref, lap_ref):
    rel = where_ref[where_at : where_at + 16, 0:1]
    ext = where_ref[where_at : where_at + 16, 1:2]

    for q in range(SZ):

        def plane(at, c):
            lanes = at * PLANE + c * SEG
            return src[src_at : src_at + 16, lanes : lanes + SEG]

        here = [plane(q + 1, c) for c in range(COMP)]
        plane_term = jnp.dot(
            jnp.concatenate(here, axis=0), lap_ref[...], preferred_element_type=F32
        )
        inside = jnp.where((q >= rel) & (q < rel + ext), -0.5, 0.0)
        orbital = [v.astype(F32) for v in here]
        fine = signed_sums(orbital)
        pot = pot_ref[q * COMP : q * COMP + COMP, :]
        back = signed_sums([fine[k] * pot[k : k + 1] for k in range(COMP)])
        for c in range(COMP):
            beside = plane(q, c).astype(F32) + plane(q + 2, c).astype(F32)
            total = plane_term[16 * c : 16 * c + 16] + back[c]
            total += orbital[c] + inside * beside
            lanes = q * PLANE + c * SEG
            dst[dst_at : dst_at + 16, lanes : lanes + SEG] = total.astype(BF16)


def fill(dst, at, src_ref, above):
    blank = jnp.zeros((16, PLANE), BF16)
    dst[at : at + 16, pl.ds(pl.multiple_of(above * PLANE, LANES), EDGE)] = src_ref[:, 0:EDGE]
    dst[at : at + 16, pl.ds(pl.multiple_of((1 - above) * EDGE, LANES), PLANE)] = blank


def last_rows(dst, dst_at, src, rows):
    lane = lax.broadcasted_iota(jnp.int32, (rows, LANES), 1)
    for j in range(2):
        for c in range(COMP):
            packed = None
            for i in range(4):
                at = PLANE + ((4 * j + i) * COMP + c) * SEG + LANES
                piece = src[0:rows, at : at + LANES].astype(F32)
                if i < 3:
                    piece = pltpu.roll(piece, 32 * (i + 1), 1)
                packed = piece if packed is None else jnp.where(lane < 32 * i, packed, piece)
            at = (j * COMP + c) * LANES
            dst[dst_at : dst_at + rows, at : at + LANES] = packed.astype(BF16)


def contract(a, b):
    return lax.dot_general(a, b, (((1,), (1,)), ((), ())), preferred_element_type=F32)


def near_kernel(
    odd_ref, chip_ref, mid_ref, where_ref, pot_ref, lap_ref, both_ref, last_ref, halo_ref, sum_ref, src
):
    fill(src, 0, chip_ref, 1 - odd_ref[0])
    src[16:32, :] = mid_ref[:, 0:FULL]
    both_ref[0:32, :] = src[:, PLANE:EDGE]
    halo_ref[0:16, :] = chip_ref[:, EDGE : EDGE + HALO]
    halo_ref[16:32, :] = mid_ref[:, FULL : FULL + HALO]
    for at in (0, 16):
        apply_planes(src, at, both_ref, 32 + at, where_ref, at, pot_ref, lap_ref)
    last_rows(last_ref, 0, src, 32)

    sum_ref[:, 0:32] = contract(both_ref[...], both_ref[0:32, :])


def near(odd, chip, mid, where, pot, laplace):
    whole = pl.BlockSpec(memory_space=pltpu.VMEM)
    return pl.pallas_call(
        near_kernel,
        in_specs=[pl.BlockSpec(memory_space=pltpu.SMEM)] + [whole] * 5,
        out_specs=[whole] * 4,
        out_shape=[
            jax.ShapeDtypeStruct((64, MAIN), BF16),
            jax.ShapeDtypeStruct((32, HALO), BF16),
            jax.ShapeDtypeStruct((32, HALO), BF16),
            jax.ShapeDtypeStruct((64, LANES), F32),
        ],
        scratch_shapes=[pltpu.VMEM((32, FULL), BF16)],
        compiler_params=params(),
        cost_estimate=SMALL,
    )(odd, chip, mid, where, pot, laplace)


def far_kernel(
    odd_ref, share_ref, across_ref, both_ref, last_ref, halo_ref, sum_ref, where_ref, pot_ref, lap_ref,
    out_ref, src, far, last, halo, sums,
):
    odd = odd_ref[0]
    fill(src, 0, across_ref, odd)
    far[0:16, :] = src[:, PLANE:EDGE]
    halo[0:32, :] = halo_ref[...]
    halo[32:48, :] = across_ref[:, EDGE : EDGE + HALO]
    last[0:32, :] = last_ref[...]
    last_rows(last, 32, src, 16)
    apply_planes(src, 0, far, 16, where_ref, 32, pot_ref, lap_ref)

    rows = contract(far[...], both_ref[0:32, :])
    column = contract(both_ref[...], far[0:16, :])
    corner = contract(far[...], far[0:16, :])
    cross = contract(last[...], halo[...]) + contract(halo[...], last[...])
    cross = jnp.where(share_ref[0] > 0, -0.5, 0.0) * cross
    sums[...] = jnp.zeros((96, LANES), F32)
    for k in range(2):
        at = 48 * k
        sums[at : at + 32, 0:32] = sum_ref[32 * k : 32 * k + 32, 0:32]
        sums[at + 32 : at + 48, 0:32] = rows[16 * k : 16 * k + 16]
        sums[at : at + 32, 32:48] = column[32 * k : 32 * k + 32]
        sums[at + 32 : at + 48, 32:48] = corner[16 * k : 16 * k + 16]
    sums[48:96, 0:48] = sums[48:96, 0:48] + cross
    lane = lax.broadcasted_iota(jnp.int32, (96, LANES), 1)
    table = sums[...]
    chip_up = pltpu.roll(table, 32, 1)
    across_down = pltpu.roll(table, LANES - 32, 1)
    even = jnp.where(lane < 16, across_down, jnp.where(lane < 32, table, chip_up))
    even = jnp.where(lane < 48, even, 0.0)
    table = jnp.where(odd > 0, table, even)
    sums[0:48, :] = table[0:48] + pltpu.roll(table[48:96], 64, 1)
    for x in range(GROUPS):
        here = odd * GROUPS + x
        there = (1 - odd) * GROUPS + x
        out_ref[here, 0:PER, :] = sums[16 + PER * x : 16 + PER * x + PER, :]
        out_ref[here, PER : 2 * PER, :] = sums[32 + PER * x : 32 + PER * x + PER, :]
        out_ref[there, 0:PER, :] = sums[PER * x : PER * x + PER, :]
        out_ref[there, PER : 2 * PER, :] = jnp.zeros((PER, LANES), F32)


def far(odd, share, across, both, last, halo, sums, where, pot, laplace):
    whole = pl.BlockSpec(memory_space=pltpu.VMEM)
    scalar = pl.BlockSpec(memory_space=pltpu.SMEM)
    return pl.pallas_call(
        far_kernel,
        in_specs=[scalar, scalar] + [whole] * 8,
        out_specs=whole,
        out_shape=jax.ShapeDtypeStruct((2 * GROUPS, 2 * PER, LANES), F32),
        scratch_shapes=[
            pltpu.VMEM((16, FULL), BF16),
            pltpu.VMEM((32, MAIN), BF16),
            pltpu.VMEM((48, HALO), BF16),
            pltpu.VMEM((48, HALO), BF16),
            pltpu.VMEM((96, LANES), F32),
        ],
        compiler_params=params(),
    )(odd, share, across, both, last, halo, sums, where, pot, laplace)


def settle_kernel(odd_ref, parts_ref, rows_ref, far_ref):
    odd = odd_ref[0]
    here, there = odd * GROUPS, (1 - odd) * GROUPS
    same, other = parts_ref[here], parts_ref[there]
    for x in range(1, GROUPS):
        same += parts_ref[here + x]
        other += parts_ref[there + x]
    rows_ref[0:8, :] = same
    rows_ref[8:16, :] = other
    far_ref[...] = same[PER:, :]


def settle(odd, parts):
    whole = pl.BlockSpec(memory_space=pltpu.VMEM)
    return pl.pallas_call(
        settle_kernel,
        in_specs=[pl.BlockSpec(memory_space=pltpu.SMEM), whole],
        out_specs=[whole] * 2,
        out_shape=[jax.ShapeDtypeStruct((16, LANES), F32), jax.ShapeDtypeStruct((PER, LANES), F32)],
        compiler_params=pltpu.CompilerParams(vmem_limit_bytes=4 * 1024 * 1024),
    )(odd, parts)


def finish_kernel(odd_ref, rows_ref, far_ref, margin_ref, ham_ref, far):
    odd = odd_ref[0] > 0
    far[...] = jnp.zeros(far.shape, F32)
    far[0:PER, :] = far_ref[...]
    own, chip, across = rows_ref[0:8, :], rows_ref[8:16, :], far[...]
    blocks = (jnp.where(odd, chip, across), own, jnp.where(odd, across, chip))
    lane = lax.broadcasted_iota(jnp.int32, (8, LANES), 1)
    for ref, first in ((margin_ref, 0), (ham_ref, 64)):
        band = jnp.zeros((8, LANES), F32)
        for k in range(3):
            turn = (16 * k - first) % LANES
            value = blocks[k] if turn == 0 else pltpu.roll(blocks[k], turn, 1)
            band += jnp.where((lane >= 16 * k) & (lane < 16 * k + 48), value, 0.0)
        ref[...] = band[0:PER, 0:80]


def finish(odd, rows, far_rows):
    whole = pl.BlockSpec(memory_space=pltpu.VMEM)
    return pl.pallas_call(
        finish_kernel,
        in_specs=[pl.BlockSpec(memory_space=pltpu.SMEM)] + [whole] * 2,
        out_specs=[whole] * 2,
        out_shape=[jax.ShapeDtypeStruct((PER, 80), F32)] * 2,
        scratch_shapes=[pltpu.VMEM((8, LANES), F32)],
        compiler_params=pltpu.CompilerParams(vmem_limit_bytes=4 * 1024 * 1024),
    )(odd, rows, far_rows)


def segment_laplace():
    cells = jnp.arange(SEG, dtype=jnp.int32)
    x, y = cells // CY, cells % CY
    step_x = jnp.abs(x[:, None] - x[None, :])
    step_y = jnp.abs(y[:, None] - y[None, :])
    return jnp.where(
        step_x + step_y == 0, 2.0, jnp.where(step_x + step_y == 1, -0.5, 0.0)
    ).astype(BF16)


def local(potential, coefficients, box_center, box_extent):
    slab = lax.axis_index("slab")
    group = lax.axis_index("grp")
    slabs = lax.axis_size("slab")
    odd = slab % 2
    on_chip = [(s, s ^ 1) for s in range(slabs)]
    across_chips = [(s, (s + 2 * (s % 2) - 1) % slabs) for s in range(slabs)]
    chips = [
        [(2 * c + k) * GROUPS + x for k in range(2) for x in range(GROUPS)] for c in range(slabs // 2)
    ]

    def frames(step):
        source = (slab + step) % slabs
        extents = lax.dynamic_slice_in_dim(box_extent, source * MEMBERS, MEMBERS)
        centers = lax.dynamic_slice_in_dim(box_center, source * MEMBERS, MEMBERS)
        return centers - source * SZ - extents // 2 + step * SZ, extents

    around = [frames(step) for step in (1 - 2 * odd, 0, 2 * odd - 1)]
    where = jnp.stack(
        [jnp.concatenate([r for r, _ in around]), jnp.concatenate([e for _, e in around])], axis=1
    )
    starts, extents = around[1]
    pot = lax.dynamic_slice_in_dim(potential, group * SEG, SEG, axis=2)
    pot = pot.reshape(SZ * COMP, SEG).astype(F32) * (1.0 / COMP)
    laplace = segment_laplace()
    share = (group < GROUPS - 1).astype(jnp.int32).reshape(1)
    flag = odd.astype(jnp.int32).reshape(1)

    got = lax.all_to_all(pack(coefficients), "grp", 0, 0, tiled=True)
    across, *placed = place(flag, starts + SZ, extents, got)
    chip, mid = place_near(flag, across, placed)
    across = lax.ppermute(across, "slab", across_chips)
    chip = lax.ppermute(chip, "slab", on_chip)
    both, last, halo, sums = near(flag, chip, mid, where, pot, laplace)
    parts = far(flag, share, across, both, last, halo, sums, where, pot, laplace)
    parts = lax.all_to_all(
        parts, ("slab", "grp"), 0, 0, tiled=True, axis_index_groups=chips
    )
    rows, far_rows = settle(flag, parts)
    return finish(flag, rows, lax.ppermute(far_rows, "slab", across_chips))


def solution(mesh):
    return jax.shard_map(
        local,
        mesh=mesh,
        in_specs=(P("slab", None, None), P(("slab", "grp"), None, None, None), P(), P()),
        out_specs=(P(("slab", "grp"), None), P(("slab", "grp"), None)),
        check_vma=False,
    )
```

```python
import jax
import jax.numpy as jnp
from jax import lax
from jax.experimental import pallas as pl
from jax.experimental.pallas import tpu as pltpu
from jax.sharding import PartitionSpec as P

GROUPS = 4
PER = 4
MEMBERS = 16
DEPTH = 16
SZ = 8
COMP = 8
CY = 32
SEG = 256
LANES = 128
PLANE = COMP * SEG
MAIN = SZ * PLANE
FULL = MAIN + PLANE
HALO = SZ * COMP * CY
STRIDE = 27 * COMP
VMEM = 20 * 1024 * 1024
F32 = jnp.float32
BF16 = jnp.bfloat16


SMALL = pl.CostEstimate(flops=1, bytes_accessed=1, transcendentals=0)


def params():
    return pltpu.CompilerParams(vmem_limit_bytes=VMEM)


def pack_kernel(in_ref, out_ref, tiles, sems):
    mains = [
        [
            pltpu.make_async_copy(
                in_ref.at[:, :, pl.ds(d * SEG + h * LANES, LANES)],
                tiles.at[d, :, pl.ds(h * 128, 128), :],
                sems.at[2 * d + h],
            )
            for h in range(2)
        ]
        for d in range(GROUPS)
    ]
    outs = [pltpu.make_async_copy(tiles.at[d], out_ref.at[d], sems.at[8 + d]) for d in range(GROUPS)]
    order = range(GROUPS - 1, -1, -1)
    for d in order:
        for copy in mains[d]:
            copy.start()
    lane = lax.broadcasted_iota(jnp.int32, (32, LANES), 1)
    for d in order:
        for copy in mains[d]:
            copy.wait()
        if d == GROUPS - 1:
            tiles[d, :, 256:288, :] = jnp.zeros((PER, 32, LANES), BF16)
        else:
            for f in range(PER):
                rows = tiles[d + 1, f, 0:128, :].astype(F32)
                tile = rows[0:32]
                for i in range(1, 4):
                    moved = pltpu.roll(rows[32 * i : 32 * i + 32], 32 * i, 1)
                    tile = jnp.where(lane < 32 * i, tile, moved)
                tiles[d, f, 256:288, :] = tile.astype(BF16)
        outs[d].start()
    for copy in outs:
        copy.wait()


def pack(coefficients):
    rows = coefficients.reshape(PER, DEPTH * COMP, GROUPS * SEG)
    return pl.pallas_call(
        pack_kernel,
        in_specs=[pl.BlockSpec(memory_space=pl.ANY)],
        out_specs=pl.BlockSpec(memory_space=pl.ANY),
        out_shape=jax.ShapeDtypeStruct((GROUPS, PER, 288, LANES), BF16),
        scratch_shapes=[
            pltpu.VMEM((GROUPS, PER, 288, LANES), BF16),
            pltpu.SemaphoreType.DMA((12,)),
        ],
        compiler_params=pltpu.CompilerParams(vmem_limit_bytes=60 * 1024 * 1024),
    )(rows)


def rows_of(frames, r):
    a = frames[pl.ds(r, 8, stride=STRIDE), :]
    b = frames[pl.ds(8 * STRIDE + r, 8, stride=STRIDE), :]
    return jnp.concatenate([a, b], axis=0)


def gather(ref, frames, first, planes, halo_first, base):
    s0, s1, sh = frames
    lane = lax.broadcasted_iota(jnp.int32, (MEMBERS, LANES), 1)
    for r in range(planes * COMP):
        for h, s in ((0, s0), (1, s1)):
            ref[:, r * SEG + h * LANES : r * SEG + h * LANES + LANES] = rows_of(s, first + r).astype(BF16)
    for j in range(2):
        for c in range(COMP):
            packed = rows_of(sh, halo_first + 4 * j * COMP + c)
            for i in range(1, 4):
                moved = pltpu.roll(rows_of(sh, halo_first + (4 * j + i) * COMP + c), 32 * i, 1)
                packed = jnp.where(lane < 32 * i, packed, moved)
            at = base + (j * COMP + c) * LANES
            ref[:, at : at + LANES] = packed.astype(BF16)


def place_kernel(odd_ref, start_ref, extent_ref, in_ref, across_ref, s0, s1, sh):
    zero = jnp.zeros((COMP, LANES), F32)
    row = lax.broadcasted_iota(jnp.int32, (128, LANES), 0)

    for n in range(MEMBERS):
        base = n * STRIDE
        start = start_ref[n]
        for i in range(11):
            blank = start + 16 + i
            blank = jnp.where(blank < 27, blank, blank - 27)
            for s in (s0, s1, sh):
                s[pl.ds(pl.multiple_of(base + blank * COMP, 8), COMP), :] = zero
        at = pl.multiple_of(base + start * COMP, 8)
        inside = row < extent_ref[n] * COMP
        s0[pl.ds(at, 128), :] = jnp.where(inside, in_ref[n, 0:128, :].astype(F32), 0.0)
        s1[pl.ds(at, 128), :] = jnp.where(inside, in_ref[n, 128:256, :].astype(F32), 0.0)
        packed = in_ref[n, 256:288, :].astype(F32)
        for i in range(4):
            part = packed if i == 0 else pltpu.roll(packed, LANES - 32 * i, 1)
            part = jnp.where(inside[32 * i : 32 * i + 32], part, 0.0)
            sh[pl.ds(pl.multiple_of(at + 32 * i, 8), 32), :] = part
    odd = odd_ref[0]
    gather(across_ref, (s0, s1, sh), odd * (15 * COMP), 8, odd * (16 * COMP), MAIN)


def place(odd, starts, extents, got):
    whole = pl.BlockSpec(memory_space=pltpu.VMEM)
    scalars = pl.BlockSpec(memory_space=pltpu.SMEM)
    return pl.pallas_call(
        place_kernel,
        in_specs=[scalars] * 3 + [whole],
        out_specs=[whole] * 4,
        out_shape=[jax.ShapeDtypeStruct((MEMBERS, MAIN + HALO), BF16)]
        + [jax.ShapeDtypeStruct((MEMBERS * STRIDE, LANES), F32)] * 3,
        compiler_params=params(),
    )(odd, starts, extents, got.reshape(MEMBERS, 288, LANES))


def place_near_kernel(odd_ref, _across, s0, s1, sh, chip_ref, mid_ref):
    even = 1 - odd_ref[0]
    gather(chip_ref, (s0, s1, sh), even * (15 * COMP), 8, even * (16 * COMP), MAIN)
    gather(mid_ref, (s0, s1, sh), 7 * COMP, 9, 8 * COMP, FULL)


def place_near(odd, across, frames):
    whole = pl.BlockSpec(memory_space=pltpu.VMEM)
    return pl.pallas_call(
        place_near_kernel,
        in_specs=[pl.BlockSpec(memory_space=pltpu.SMEM), pl.BlockSpec(memory_space=pl.ANY)] + [whole] * 3,
        out_specs=[whole] * 2,
        out_shape=[
            jax.ShapeDtypeStruct((MEMBERS, MAIN + HALO), BF16),
            jax.ShapeDtypeStruct((MEMBERS, FULL + HALO), BF16),
        ],
        compiler_params=params(),
        cost_estimate=SMALL,
    )(odd, across, *frames)


def signed_sums(values):
    values = list(values)
    for bit in (1, 2, 4):
        values = [
            values[k ^ bit] - values[k] if k & bit else values[k] + values[k ^ bit]
            for k in range(COMP)
        ]
    return values


def apply_planes(src, src_at, dst, dst_at, where_ref, where_at, pot_ref, lap_ref):
    rel = where_ref[where_at : where_at + 16, 0:1]
    ext = where_ref[where_at : where_at + 16, 1:2]

    def plane(q, c):
        lanes = (q + 1) * PLANE + c * SEG
        return src[src_at : src_at + 16, lanes : lanes + SEG]

    for q in range(-1, SZ):
        inside = jnp.where((q >= rel) & (q < rel + ext), -0.5, 0.0)
        if q < 0:
            totals = [inside * plane(0, c).astype(F32) for c in range(COMP)]
        else:
            here = [plane(q, c) for c in range(COMP)]
            plane_term = jnp.dot(
                jnp.concatenate(here, axis=0), lap_ref[...], preferred_element_type=F32
            )
            orbital = [v.astype(F32) for v in here]
            fine = signed_sums(orbital)
            pot = pot_ref[q * COMP : q * COMP + COMP, :]
            back = signed_sums([fine[k] * pot[k : k + 1] for k in range(COMP)])
            totals = []
            for c in range(COMP):
                beside = plane(q - 1, c).astype(F32)
                if q < SZ - 1:
                    beside += plane(q + 1, c).astype(F32)
                total = plane_term[16 * c : 16 * c + 16] + back[c]
                totals.append(total + orbital[c] + inside * beside)
        for c in range(COMP):
            lanes = (q + 1) * PLANE + c * SEG
            dst[dst_at : dst_at + 16, lanes : lanes + SEG] = totals[c].astype(BF16)


def fill(dst, at, src_ref, above):
    blank = jnp.zeros((16, PLANE), BF16)
    dst[at : at + 16, pl.ds(pl.multiple_of(above * PLANE, LANES), MAIN)] = src_ref[:, 0:MAIN]
    dst[at : at + 16, pl.ds(pl.multiple_of((1 - above) * MAIN, LANES), PLANE)] = blank


def last_rows(dst, dst_at, src, rows):
    lane = lax.broadcasted_iota(jnp.int32, (rows, LANES), 1)
    for j in range(2):
        for c in range(COMP):
            packed = None
            for i in range(4):
                at = PLANE + ((4 * j + i) * COMP + c) * SEG + LANES
                piece = src[0:rows, at : at + LANES].astype(F32)
                if i < 3:
                    piece = pltpu.roll(piece, 32 * (i + 1), 1)
                packed = piece if packed is None else jnp.where(lane < 32 * i, packed, piece)
            at = (j * COMP + c) * LANES
            dst[dst_at : dst_at + rows, at : at + LANES] = packed.astype(BF16)


def contract(a, b):
    return lax.dot_general(a, b, (((1,), (1,)), ((), ())), preferred_element_type=F32)


def near_kernel(odd_ref, chip_ref, mid_ref, where_ref, pot_ref, lap_ref, both_ref, last_ref, halo_ref, sum_ref):
    fill(both_ref, 0, chip_ref, 1 - odd_ref[0])
    both_ref[16:32, :] = mid_ref[:, 0:FULL]
    halo_ref[0:16, :] = chip_ref[:, MAIN : MAIN + HALO]
    halo_ref[16:32, :] = mid_ref[:, FULL : FULL + HALO]
    for at in (0, 16):
        apply_planes(both_ref, at, both_ref, 32 + at, where_ref, at, pot_ref, lap_ref)
    last_rows(last_ref, 0, both_ref, 32)
    sums = contract(both_ref[:, PLANE:FULL], both_ref[0:32, PLANE:FULL])
    sum_ref[0:32, 0:32] = sums[0:32]
    sum_ref[32:64, 0:32] = sums[32:64] + contract(both_ref[32:64, 0:PLANE], both_ref[0:32, 0:PLANE])


def near(odd, chip, mid, where, pot, laplace):
    whole = pl.BlockSpec(memory_space=pltpu.VMEM)
    return pl.pallas_call(
        near_kernel,
        in_specs=[pl.BlockSpec(memory_space=pltpu.SMEM)] + [whole] * 5,
        out_specs=[whole] * 4,
        out_shape=[
            jax.ShapeDtypeStruct((64, FULL), BF16),
            jax.ShapeDtypeStruct((32, HALO), BF16),
            jax.ShapeDtypeStruct((32, HALO), BF16),
            jax.ShapeDtypeStruct((64, LANES), F32),
        ],
        compiler_params=params(),
        cost_estimate=SMALL,
    )(odd, chip, mid, where, pot, laplace)


def far_kernel(
    odd_ref, share_ref, across_ref, both_ref, last_ref, halo_ref, sum_ref, where_ref, pot_ref, lap_ref,
    out_ref, far, last, halo, sums,
):
    odd = odd_ref[0]
    fill(far, 0, across_ref, odd)
    halo[0:32, :] = halo_ref[...]
    halo[32:48, :] = across_ref[:, MAIN : MAIN + HALO]
    last[0:32, :] = last_ref[...]
    last_rows(last, 32, far, 16)
    apply_planes(far, 0, far, 16, where_ref, 32, pot_ref, lap_ref)
    main, below = slice(PLANE, FULL), slice(0, PLANE)
    rows = contract(far[:, main], both_ref[0:32, main])
    column = contract(both_ref[:, main], far[0:16, main])
    corner = contract(far[:, main], far[0:16, main])
    rows_below = contract(far[16:32, below], both_ref[0:32, below])
    column_below = contract(both_ref[32:64, below], far[0:16, below])
    corner_below = contract(far[16:32, below], far[0:16, below])
    rows = (rows[0:16], rows[16:32] + rows_below)
    column = (column[0:32], column[32:64] + column_below)
    corner = (corner[0:16], corner[16:32] + corner_below)
    cross = contract(last[...], halo[...]) + contract(halo[...], last[...])
    cross = jnp.where(share_ref[0] > 0, -0.5, 0.0) * cross
    sums[...] = jnp.zeros((96, LANES), F32)
    for k in range(2):
        at = 48 * k
        sums[at : at + 32, 0:32] = sum_ref[32 * k : 32 * k + 32, 0:32]
        sums[at + 32 : at + 48, 0:32] = rows[k]
        sums[at : at + 32, 32:48] = column[k]
        sums[at + 32 : at + 48, 32:48] = corner[k]
    sums[48:96, 0:48] = sums[48:96, 0:48] + cross
    lane = lax.broadcasted_iota(jnp.int32, (96, LANES), 1)
    table = sums[...]
    chip_up = pltpu.roll(table, 32, 1)
    across_down = pltpu.roll(table, LANES - 32, 1)
    even = jnp.where(lane < 16, across_down, jnp.where(lane < 32, table, chip_up))
    even = jnp.where(lane < 48, even, 0.0)
    table = jnp.where(odd > 0, table, even)
    sums[0:48, :] = table[0:48] + pltpu.roll(table[48:96], 64, 1)
    for x in range(GROUPS):
        here = odd * GROUPS + x
        there = (1 - odd) * GROUPS + x
        out_ref[here, 0:PER, :] = sums[16 + PER * x : 16 + PER * x + PER, :]
        out_ref[here, PER : 2 * PER, :] = sums[32 + PER * x : 32 + PER * x + PER, :]
        out_ref[there, 0:PER, :] = sums[PER * x : PER * x + PER, :]
        out_ref[there, PER : 2 * PER, :] = jnp.zeros((PER, LANES), F32)


def far(odd, share, across, both, last, halo, sums, where, pot, laplace):
    whole = pl.BlockSpec(memory_space=pltpu.VMEM)
    scalar = pl.BlockSpec(memory_space=pltpu.SMEM)
    return pl.pallas_call(
        far_kernel,
        in_specs=[scalar, scalar] + [whole] * 8,
        out_specs=whole,
        out_shape=jax.ShapeDtypeStruct((2 * GROUPS, 2 * PER, LANES), F32),
        scratch_shapes=[
            pltpu.VMEM((32, FULL), BF16),
            pltpu.VMEM((48, HALO), BF16),
            pltpu.VMEM((48, HALO), BF16),
            pltpu.VMEM((96, LANES), F32),
        ],
        compiler_params=params(),
    )(odd, share, across, both, last, halo, sums, where, pot, laplace)


def settle_kernel(odd_ref, parts_ref, rows_ref, far_ref):
    odd = odd_ref[0]
    here, there = odd * GROUPS, (1 - odd) * GROUPS
    same, other = parts_ref[here], parts_ref[there]
    for x in range(1, GROUPS):
        same += parts_ref[here + x]
        other += parts_ref[there + x]
    rows_ref[0:8, :] = same
    rows_ref[8:16, :] = other
    far_ref[...] = same[PER:, :]


def settle(odd, parts):
    whole = pl.BlockSpec(memory_space=pltpu.VMEM)
    return pl.pallas_call(
        settle_kernel,
        in_specs=[pl.BlockSpec(memory_space=pltpu.SMEM), whole],
        out_specs=[whole] * 2,
        out_shape=[jax.ShapeDtypeStruct((16, LANES), F32), jax.ShapeDtypeStruct((PER, LANES), F32)],
        compiler_params=pltpu.CompilerParams(vmem_limit_bytes=4 * 1024 * 1024),
    )(odd, parts)


def finish_kernel(odd_ref, rows_ref, far_ref, margin_ref, ham_ref, far):
    odd = odd_ref[0] > 0
    far[...] = jnp.zeros(far.shape, F32)
    far[0:PER, :] = far_ref[...]
    own, chip, across = rows_ref[0:8, :], rows_ref[8:16, :], far[...]
    blocks = (jnp.where(odd, chip, across), own, jnp.where(odd, across, chip))
    lane = lax.broadcasted_iota(jnp.int32, (8, LANES), 1)
    for ref, first in ((margin_ref, 0), (ham_ref, 64)):
        band = jnp.zeros((8, LANES), F32)
        for k in range(3):
            turn = (16 * k - first) % LANES
            value = blocks[k] if turn == 0 else pltpu.roll(blocks[k], turn, 1)
            band += jnp.where((lane >= 16 * k) & (lane < 16 * k + 48), value, 0.0)
        ref[...] = band[0:PER, 0:80]


def finish(odd, rows, far_rows):
    whole = pl.BlockSpec(memory_space=pltpu.VMEM)
    return pl.pallas_call(
        finish_kernel,
        in_specs=[pl.BlockSpec(memory_space=pltpu.SMEM)] + [whole] * 2,
        out_specs=[whole] * 2,
        out_shape=[jax.ShapeDtypeStruct((PER, 80), F32)] * 2,
        scratch_shapes=[pltpu.VMEM((8, LANES), F32)],
        compiler_params=pltpu.CompilerParams(vmem_limit_bytes=4 * 1024 * 1024),
    )(odd, rows, far_rows)


def segment_laplace():
    cells = jnp.arange(SEG, dtype=jnp.int32)
    x, y = cells // CY, cells % CY
    step_x = jnp.abs(x[:, None] - x[None, :])
    step_y = jnp.abs(y[:, None] - y[None, :])
    return jnp.where(
        step_x + step_y == 0, 2.0, jnp.where(step_x + step_y == 1, -0.5, 0.0)
    ).astype(BF16)


def local(potential, coefficients, box_center, box_extent):
    slab = lax.axis_index("slab")
    group = lax.axis_index("grp")
    slabs = lax.axis_size("slab")
    odd = slab % 2
    on_chip = [(s, s ^ 1) for s in range(slabs)]
    across_chips = [(s, (s + 2 * (s % 2) - 1) % slabs) for s in range(slabs)]
    chips = [
        [(2 * c + k) * GROUPS + x for k in range(2) for x in range(GROUPS)] for c in range(slabs // 2)
    ]

    def frames(step):
        source = (slab + step) % slabs
        extents = lax.dynamic_slice_in_dim(box_extent, source * MEMBERS, MEMBERS)
        centers = lax.dynamic_slice_in_dim(box_center, source * MEMBERS, MEMBERS)
        return centers - source * SZ - extents // 2 + step * SZ, extents

    around = [frames(step) for step in (1 - 2 * odd, 0, 2 * odd - 1)]
    where = jnp.stack(
        [jnp.concatenate([r for r, _ in around]), jnp.concatenate([e for _, e in around])], axis=1
    )
    starts, extents = around[1]
    pot = lax.dynamic_slice_in_dim(potential, group * SEG, SEG, axis=2)
    pot = pot.reshape(SZ * COMP, SEG).astype(F32) * (1.0 / COMP)
    laplace = segment_laplace()
    share = (group < GROUPS - 1).astype(jnp.int32).reshape(1)
    flag = odd.astype(jnp.int32).reshape(1)

    got = lax.all_to_all(pack(coefficients), "grp", 0, 0, tiled=True)
    across, *placed = place(flag, starts + SZ, extents, got)
    chip, mid = place_near(flag, across, placed)
    across = lax.ppermute(across, "slab", across_chips)
    chip = lax.ppermute(chip, "slab", on_chip)
    both, last, halo, sums = near(flag, chip, mid, where, pot, laplace)
    parts = far(flag, share, across, both, last, halo, sums, where, pot, laplace)
    parts = lax.all_to_all(
        parts, ("slab", "grp"), 0, 0, tiled=True, axis_index_groups=chips
    )
    rows, far_rows = settle(flag, parts)
    return finish(flag, rows, lax.ppermute(far_rows, "slab", across_chips))


def solution(mesh):
    return jax.shard_map(
        local,
        mesh=mesh,
        in_specs=(P("slab", None, None), P(("slab", "grp"), None, None, None), P(), P()),
        out_specs=(P(("slab", "grp"), None), P(("slab", "grp"), None)),
        check_vma=False,
    )
```

```python
import jax
import jax.numpy as jnp
from jax import lax
from jax.experimental import pallas as pl
from jax.experimental.pallas import tpu as pltpu
from jax.sharding import PartitionSpec as P

GROUPS = 4
PER = 4
MEMBERS = 16
DEPTH = 16
SZ = 8
COMP = 8
CY = 32
SEG = 256
LANES = 128
PLANE = COMP * SEG
MAIN = SZ * PLANE
FULL = MAIN + PLANE
HALO = SZ * COMP * CY
STRIDE = 27 * COMP
VMEM = 20 * 1024 * 1024
F32 = jnp.float32
BF16 = jnp.bfloat16


SMALL = pl.CostEstimate(flops=1, bytes_accessed=1, transcendentals=0)


def params():
    return pltpu.CompilerParams(vmem_limit_bytes=VMEM)


def pack_kernel(in_ref, out_ref, tiles, sems):
    mains = [
        [
            pltpu.make_async_copy(
                in_ref.at[:, :, pl.ds(d * SEG + h * LANES, LANES)],
                tiles.at[d, :, pl.ds(h * 128, 128), :],
                sems.at[2 * d + h],
            )
            for h in range(2)
        ]
        for d in range(GROUPS)
    ]
    outs = [pltpu.make_async_copy(tiles.at[d], out_ref.at[d], sems.at[8 + d]) for d in range(GROUPS)]
    order = range(GROUPS - 1, -1, -1)
    for d in order:
        for copy in mains[d]:
            copy.start()
    lane = lax.broadcasted_iota(jnp.int32, (32, LANES), 1)
    for d in order:
        for copy in mains[d]:
            copy.wait()
        if d == GROUPS - 1:
            tiles[d, :, 256:288, :] = jnp.zeros((PER, 32, LANES), BF16)
        else:
            for f in range(PER):
                rows = tiles[d + 1, f, 0:128, :].astype(F32)
                tile = rows[0:32]
                for i in range(1, 4):
                    moved = pltpu.roll(rows[32 * i : 32 * i + 32], 32 * i, 1)
                    tile = jnp.where(lane < 32 * i, tile, moved)
                tiles[d, f, 256:288, :] = tile.astype(BF16)
        outs[d].start()
    for copy in outs:
        copy.wait()


def pack(coefficients):
    rows = coefficients.reshape(PER, DEPTH * COMP, GROUPS * SEG)
    return pl.pallas_call(
        pack_kernel,
        in_specs=[pl.BlockSpec(memory_space=pl.ANY)],
        out_specs=pl.BlockSpec(memory_space=pl.ANY),
        out_shape=jax.ShapeDtypeStruct((GROUPS, PER, 288, LANES), BF16),
        scratch_shapes=[
            pltpu.VMEM((GROUPS, PER, 288, LANES), BF16),
            pltpu.SemaphoreType.DMA((12,)),
        ],
        compiler_params=pltpu.CompilerParams(vmem_limit_bytes=60 * 1024 * 1024),
    )(rows)


def rows_of(frames, r):
    a = frames[pl.ds(r, 8, stride=STRIDE), :]
    b = frames[pl.ds(8 * STRIDE + r, 8, stride=STRIDE), :]
    return jnp.concatenate([a, b], axis=0)


def gather(ref, frames, box_ref, first, planes):
    s0, s1, _ = frames
    lane = lax.broadcasted_iota(jnp.int32, (MEMBERS, LANES), 1)
    start = jnp.broadcast_to(box_ref[:, 0:1], (MEMBERS, LANES))
    extent = jnp.broadcast_to(box_ref[:, 1:2], (MEMBERS, LANES))

    def inside(f):
        return (f >= start) & (f < start + extent)

    for q in range(planes):
        keep = inside(first + q)
        for c in range(COMP):
            for h, s in ((0, s0), (1, s1)):
                at = (q * COMP + c) * SEG + h * LANES
                tile = rows_of(s, (first + q) * COMP + c)
                ref[:, at : at + LANES] = jnp.where(keep, tile, 0.0).astype(BF16)
    return lane, inside


def gather_after(ref, sh, lane, inside, first, base):
    for j in range(2):
        planes = [first + 4 * j + i for i in range(4)]
        keep = inside(planes[0] + lane // CY)
        for c in range(COMP):
            packed = rows_of(sh, planes[0] * COMP + c)
            for i in range(1, 4):
                moved = pltpu.roll(rows_of(sh, planes[i] * COMP + c), 32 * i, 1)
                packed = jnp.where(lane < 32 * i, packed, moved)
            at = base + (j * COMP + c) * LANES
            ref[:, at : at + LANES] = jnp.where(keep, packed, 0.0).astype(BF16)


def place_kernel(odd_ref, start_ref, box_ref, in_ref, across_ref, s0, s1, sh):
    for n in range(MEMBERS):
        at = pl.multiple_of(n * STRIDE + start_ref[n] * COMP, 8)
        s0[pl.ds(at, 128), :] = in_ref[n, 0:128, :].astype(F32)
        s1[pl.ds(at, 128), :] = in_ref[n, 128:256, :].astype(F32)
        packed = in_ref[n, 256:288, :].astype(F32)
        for i in range(4):
            part = packed if i == 0 else pltpu.roll(packed, LANES - 32 * i, 1)
            sh[pl.ds(pl.multiple_of(at + 32 * i, 8), 32), :] = part
    odd = odd_ref[0]
    lane, inside = gather(across_ref, (s0, s1, sh), box_ref, odd * 15, 8)
    gather_after(across_ref, sh, lane, inside, odd * 16, MAIN)


def place(odd, starts, box, got):
    whole = pl.BlockSpec(memory_space=pltpu.VMEM)
    scalars = pl.BlockSpec(memory_space=pltpu.SMEM)
    return pl.pallas_call(
        place_kernel,
        in_specs=[scalars] * 2 + [whole] * 2,
        out_specs=[whole] * 4,
        out_shape=[jax.ShapeDtypeStruct((MEMBERS, MAIN + HALO), BF16)]
        + [jax.ShapeDtypeStruct((MEMBERS * STRIDE, LANES), F32)] * 3,
        compiler_params=params(),
    )(odd, starts, box, got.reshape(MEMBERS, 288, LANES))


def place_near_kernel(odd_ref, box_ref, _across, s0, s1, sh, chip_ref, mid_ref):
    even = 1 - odd_ref[0]
    frames = (s0, s1, sh)
    lane, inside = gather(chip_ref, frames, box_ref, even * 15, 8)
    gather_after(chip_ref, sh, lane, inside, even * 16, MAIN)
    gather(mid_ref, frames, box_ref, 7, 9)
    gather_after(mid_ref, sh, lane, inside, 8, FULL)


def place_near(odd, box, across, frames):
    whole = pl.BlockSpec(memory_space=pltpu.VMEM)
    return pl.pallas_call(
        place_near_kernel,
        in_specs=[pl.BlockSpec(memory_space=pltpu.SMEM), whole, pl.BlockSpec(memory_space=pl.ANY)] + [whole] * 3,
        out_specs=[whole] * 2,
        out_shape=[
            jax.ShapeDtypeStruct((MEMBERS, MAIN + HALO), BF16),
            jax.ShapeDtypeStruct((MEMBERS, FULL + HALO), BF16),
        ],
        compiler_params=params(),
        cost_estimate=SMALL,
    )(odd, box, across, *frames)


def signed_sums(values):
    values = list(values)
    for bit in (1, 2, 4):
        values = [
            values[k ^ bit] - values[k] if k & bit else values[k] + values[k ^ bit]
            for k in range(COMP)
        ]
    return values


def apply_planes(src, src_at, dst, dst_at, where_ref, where_at, pot_ref, lap_ref):
    rel = where_ref[where_at : where_at + 16, 0:1]
    ext = where_ref[where_at : where_at + 16, 1:2]

    def plane(q, c):
        lanes = (q + 1) * PLANE + c * SEG
        return src[src_at : src_at + 16, lanes : lanes + SEG]

    for q in range(-1, SZ):
        inside = jnp.where((q >= rel) & (q < rel + ext), -0.5, 0.0)
        if q < 0:
            totals = [inside * plane(0, c).astype(F32) for c in range(COMP)]
        else:
            here = [plane(q, c) for c in range(COMP)]
            plane_term = jnp.dot(
                jnp.concatenate(here, axis=0), lap_ref[...], preferred_element_type=F32
            )
            orbital = [v.astype(F32) for v in here]
            fine = signed_sums(orbital)
            pot = pot_ref[q * COMP : q * COMP + COMP, :]
            back = signed_sums([fine[k] * pot[k : k + 1] for k in range(COMP)])
            totals = []
            for c in range(COMP):
                beside = plane(q - 1, c).astype(F32)
                if q < SZ - 1:
                    beside += plane(q + 1, c).astype(F32)
                total = plane_term[16 * c : 16 * c + 16] + back[c]
                totals.append(total + inside * beside)
        for c in range(COMP):
            lanes = (q + 1) * PLANE + c * SEG
            dst[dst_at : dst_at + 16, lanes : lanes + SEG] = totals[c].astype(BF16)


def fill(dst, at, src_ref, above):
    blank = jnp.zeros((16, PLANE), BF16)
    dst[at : at + 16, pl.ds(pl.multiple_of(above * PLANE, LANES), MAIN)] = src_ref[:, 0:MAIN]
    dst[at : at + 16, pl.ds(pl.multiple_of((1 - above) * MAIN, LANES), PLANE)] = blank


def last_rows(dst, dst_at, src, rows):
    lane = lax.broadcasted_iota(jnp.int32, (rows, LANES), 1)
    for j in range(2):
        for c in range(COMP):
            packed = None
            for i in range(4):
                at = PLANE + ((4 * j + i) * COMP + c) * SEG + LANES
                piece = src[0:rows, at : at + LANES].astype(F32)
                if i < 3:
                    piece = pltpu.roll(piece, 32 * (i + 1), 1)
                packed = piece if packed is None else jnp.where(lane < 32 * i, packed, piece)
            at = (j * COMP + c) * LANES
            dst[dst_at : dst_at + rows, at : at + LANES] = packed.astype(BF16)


def contract(a, b):
    return lax.dot_general(a, b, (((1,), (1,)), ((), ())), preferred_element_type=F32)


def near_kernel(odd_ref, chip_ref, mid_ref, where_ref, pot_ref, lap_ref, both_ref, last_ref, halo_ref, sum_ref):
    fill(both_ref, 0, chip_ref, 1 - odd_ref[0])
    both_ref[16:32, :] = mid_ref[:, 0:FULL]
    halo_ref[0:16, :] = chip_ref[:, MAIN : MAIN + HALO]
    halo_ref[16:32, :] = mid_ref[:, FULL : FULL + HALO]
    for at in (0, 16):
        apply_planes(both_ref, at, both_ref, 32 + at, where_ref, at, pot_ref, lap_ref)
    last_rows(last_ref, 0, both_ref, 32)
    sums = contract(both_ref[:, PLANE:FULL], both_ref[0:32, PLANE:FULL])
    sum_ref[0:32, 0:32] = sums[0:32]
    sum_ref[32:64, 0:32] = sums[32:64] + contract(both_ref[32:64, 0:PLANE], both_ref[0:32, 0:PLANE])


def near(odd, chip, mid, where, pot, laplace):
    whole = pl.BlockSpec(memory_space=pltpu.VMEM)
    return pl.pallas_call(
        near_kernel,
        in_specs=[pl.BlockSpec(memory_space=pltpu.SMEM)] + [whole] * 5,
        out_specs=[whole] * 4,
        out_shape=[
            jax.ShapeDtypeStruct((64, FULL), BF16),
            jax.ShapeDtypeStruct((32, HALO), BF16),
            jax.ShapeDtypeStruct((32, HALO), BF16),
            jax.ShapeDtypeStruct((64, LANES), F32),
        ],
        compiler_params=params(),
        cost_estimate=SMALL,
    )(odd, chip, mid, where, pot, laplace)


def far_kernel(
    odd_ref, share_ref, across_ref, both_ref, last_ref, halo_ref, sum_ref, where_ref, pot_ref, lap_ref,
    out_ref, far, last, halo, sums, turn,
):
    odd = odd_ref[0]
    fill(far, 0, across_ref, odd)
    halo[0:32, :] = halo_ref[...]
    halo[32:48, :] = across_ref[:, MAIN : MAIN + HALO]
    last[0:32, :] = last_ref[...]
    last_rows(last, 32, far, 16)
    apply_planes(far, 0, far, 16, where_ref, 32, pot_ref, lap_ref)
    main, below = slice(PLANE, FULL), slice(0, PLANE)
    table = contract(jnp.concatenate([both_ref[:, main], far[:, main]], axis=0), far[:, main])
    below_table = contract(jnp.concatenate([both_ref[:, below], far[:, below]], axis=0), far[:, below])
    cols = lax.broadcasted_iota(jnp.int32, (32, 32), 1)
    turn[...] = jnp.zeros((LANES, LANES), F32)
    turn[0:32, 0:32] = table[0:32] + jnp.where(cols >= 16, below_table[0:32], 0.0)
    turned = turn[...].T
    rows = (turned[0:16, 0:32], turned[16:32, 0:32])
    column = (table[0:32, 0:16], table[32:64, 0:16] + below_table[32:64, 0:16])
    corner = (table[64:80, 0:16], table[80:96, 0:16] + below_table[80:96, 0:16])
    cross = contract(last[...], halo[...]) + contract(halo[...], last[...])
    cross = jnp.where(share_ref[0] > 0, -0.5, 0.0) * cross
    sums[...] = jnp.zeros((96, LANES), F32)
    for k in range(2):
        at = 48 * k
        sums[at : at + 32, 0:32] = sum_ref[32 * k : 32 * k + 32, 0:32]
        sums[at + 32 : at + 48, 0:32] = rows[k]
        sums[at : at + 32, 32:48] = column[k]
        sums[at + 32 : at + 48, 32:48] = corner[k]
    sums[48:96, 0:48] = sums[48:96, 0:48] + cross
    lane = lax.broadcasted_iota(jnp.int32, (96, LANES), 1)
    table = sums[...]
    chip_up = pltpu.roll(table, 32, 1)
    across_down = pltpu.roll(table, LANES - 32, 1)
    even = jnp.where(lane < 16, across_down, jnp.where(lane < 32, table, chip_up))
    even = jnp.where(lane < 48, even, 0.0)
    table = jnp.where(odd > 0, table, even)
    sums[0:48, :] = table[0:48] + pltpu.roll(table[48:96], 64, 1)
    for x in range(GROUPS):
        here = odd * GROUPS + x
        there = (1 - odd) * GROUPS + x
        out_ref[here, 0:PER, :] = sums[16 + PER * x : 16 + PER * x + PER, :]
        out_ref[here, PER : 2 * PER, :] = sums[32 + PER * x : 32 + PER * x + PER, :]
        out_ref[there, 0:PER, :] = sums[PER * x : PER * x + PER, :]
        out_ref[there, PER : 2 * PER, :] = jnp.zeros((PER, LANES), F32)


def far(odd, share, across, both, last, halo, sums, where, pot, laplace):
    whole = pl.BlockSpec(memory_space=pltpu.VMEM)
    scalar = pl.BlockSpec(memory_space=pltpu.SMEM)
    return pl.pallas_call(
        far_kernel,
        in_specs=[scalar, scalar] + [whole] * 8,
        out_specs=whole,
        out_shape=jax.ShapeDtypeStruct((2 * GROUPS, 2 * PER, LANES), F32),
        scratch_shapes=[
            pltpu.VMEM((32, FULL), BF16),
            pltpu.VMEM((48, HALO), BF16),
            pltpu.VMEM((48, HALO), BF16),
            pltpu.VMEM((96, LANES), F32),
            pltpu.VMEM((LANES, LANES), F32),
        ],
        compiler_params=params(),
    )(odd, share, across, both, last, halo, sums, where, pot, laplace)


def settle_kernel(odd_ref, parts_ref, rows_ref, far_ref):
    odd = odd_ref[0]
    here, there = odd * GROUPS, (1 - odd) * GROUPS
    same, other = parts_ref[here], parts_ref[there]
    for x in range(1, GROUPS):
        same += parts_ref[here + x]
        other += parts_ref[there + x]
    rows_ref[0:8, :] = same
    rows_ref[8:16, :] = other
    far_ref[...] = same[PER:, :]


def settle(odd, parts):
    whole = pl.BlockSpec(memory_space=pltpu.VMEM)
    return pl.pallas_call(
        settle_kernel,
        in_specs=[pl.BlockSpec(memory_space=pltpu.SMEM), whole],
        out_specs=[whole] * 2,
        out_shape=[jax.ShapeDtypeStruct((16, LANES), F32), jax.ShapeDtypeStruct((PER, LANES), F32)],
        compiler_params=pltpu.CompilerParams(vmem_limit_bytes=4 * 1024 * 1024),
    )(odd, parts)


def finish_kernel(odd_ref, rows_ref, far_ref, margin_ref, ham_ref, far):
    odd = odd_ref[0] > 0
    far[...] = jnp.zeros(far.shape, F32)
    far[0:PER, :] = far_ref[...]
    own, chip, across = rows_ref[0:8, :], rows_ref[8:16, :], far[...]
    blocks = (jnp.where(odd, chip, across), own, jnp.where(odd, across, chip))
    lane = lax.broadcasted_iota(jnp.int32, (8, LANES), 1)
    for ref, first in ((margin_ref, 0), (ham_ref, 64)):
        band = jnp.zeros((8, LANES), F32)
        for k in range(3):
            turn = (16 * k - first) % LANES
            value = blocks[k] if turn == 0 else pltpu.roll(blocks[k], turn, 1)
            band += jnp.where((lane >= 16 * k) & (lane < 16 * k + 48), value, 0.0)
        ref[...] = band[0:PER, 0:80]


def finish(odd, rows, far_rows):
    whole = pl.BlockSpec(memory_space=pltpu.VMEM)
    return pl.pallas_call(
        finish_kernel,
        in_specs=[pl.BlockSpec(memory_space=pltpu.SMEM)] + [whole] * 2,
        out_specs=[whole] * 2,
        out_shape=[jax.ShapeDtypeStruct((PER, 80), F32)] * 2,
        scratch_shapes=[pltpu.VMEM((8, LANES), F32)],
        compiler_params=pltpu.CompilerParams(vmem_limit_bytes=4 * 1024 * 1024),
    )(odd, rows, far_rows)


def segment_laplace():
    cells = jnp.arange(SEG, dtype=jnp.int32)
    x, y = cells // CY, cells % CY
    step_x = jnp.abs(x[:, None] - x[None, :])
    step_y = jnp.abs(y[:, None] - y[None, :])
    return jnp.where(
        step_x + step_y == 0, 3.0, jnp.where(step_x + step_y == 1, -0.5, 0.0)
    ).astype(BF16)


def local(potential, coefficients, box_center, box_extent):
    slab = lax.axis_index("slab")
    group = lax.axis_index("grp")
    slabs = lax.axis_size("slab")
    odd = slab % 2
    on_chip = [(s, s ^ 1) for s in range(slabs)]
    across_chips = [(s, (s + 2 * (s % 2) - 1) % slabs) for s in range(slabs)]
    chips = [
        [(2 * c + k) * GROUPS + x for k in range(2) for x in range(GROUPS)] for c in range(slabs // 2)
    ]

    def frames(step):
        source = (slab + step) % slabs
        extents = lax.dynamic_slice_in_dim(box_extent, source * MEMBERS, MEMBERS)
        centers = lax.dynamic_slice_in_dim(box_center, source * MEMBERS, MEMBERS)
        return centers - source * SZ - extents // 2 + step * SZ, extents

    around = [frames(step) for step in (1 - 2 * odd, 0, 2 * odd - 1)]
    where = jnp.stack(
        [jnp.concatenate([r for r, _ in around]), jnp.concatenate([e for _, e in around])], axis=1
    )
    starts, extents = around[1]
    pot = lax.dynamic_slice_in_dim(potential, group * SEG, SEG, axis=2)
    pot = pot.reshape(SZ * COMP, SEG).astype(F32) * (1.0 / COMP)
    laplace = segment_laplace()
    share = (group < GROUPS - 1).astype(jnp.int32).reshape(1)
    flag = odd.astype(jnp.int32).reshape(1)

    got = lax.all_to_all(pack(coefficients), "grp", 0, 0, tiled=True)
    box = jnp.stack([starts + SZ, extents], axis=1)
    across, *placed = place(flag, starts + SZ, box, got)
    chip, mid = place_near(flag, box, across, placed)
    across = lax.ppermute(across, "slab", across_chips)
    chip = lax.ppermute(chip, "slab", on_chip)
    both, last, halo, sums = near(flag, chip, mid, where, pot, laplace)
    parts = far(flag, share, across, both, last, halo, sums, where, pot, laplace)
    parts = lax.all_to_all(
        parts, ("slab", "grp"), 0, 0, tiled=True, axis_index_groups=chips
    )
    rows, far_rows = settle(flag, parts)
    return finish(flag, rows, lax.ppermute(far_rows, "slab", across_chips))


def solution(mesh):
    return jax.shard_map(
        local,
        mesh=mesh,
        in_specs=(P("slab", None, None), P(("slab", "grp"), None, None, None), P(), P()),
        out_specs=(P(("slab", "grp"), None), P(("slab", "grp"), None)),
        check_vma=False,
    )
```

```python
import jax
import jax.numpy as jnp
from jax import lax
from jax.experimental import pallas as pl
from jax.experimental.pallas import tpu as pltpu
from jax.sharding import PartitionSpec as P

GROUPS = 4
PER = 4
MEMBERS = 16
DEPTH = 16
SZ = 8
COMP = 8
CY = 32
SEG = 256
LANES = 128
PLANE = COMP * SEG
MAIN = SZ * PLANE
FULL = MAIN + PLANE
HALO = SZ * COMP * CY
STRIDE = 27 * COMP
VMEM = 20 * 1024 * 1024
F32 = jnp.float32
BF16 = jnp.bfloat16


SMALL = pl.CostEstimate(flops=1, bytes_accessed=1, transcendentals=0)


def params():
    return pltpu.CompilerParams(vmem_limit_bytes=VMEM)


def pack_kernel(in_ref, out_ref, tiles, sems):
    mains = [
        [
            pltpu.make_async_copy(
                in_ref.at[:, :, pl.ds(d * SEG + h * LANES, LANES)],
                tiles.at[d, :, pl.ds(h * 128, 128), :],
                sems.at[2 * d + h],
            )
            for h in range(2)
        ]
        for d in range(GROUPS)
    ]
    outs = [pltpu.make_async_copy(tiles.at[d], out_ref.at[d], sems.at[8 + d]) for d in range(GROUPS)]
    order = range(GROUPS - 1, -1, -1)
    for d in order:
        for copy in mains[d]:
            copy.start()
    lane = lax.broadcasted_iota(jnp.int32, (32, LANES), 1)
    for d in order:
        for copy in mains[d]:
            copy.wait()
        if d == GROUPS - 1:
            tiles[d, :, 256:288, :] = jnp.zeros((PER, 32, LANES), BF16)
        else:
            for f in range(PER):
                rows = tiles[d + 1, f, 0:128, :].astype(F32)
                tile = rows[0:32]
                for i in range(1, 4):
                    moved = pltpu.roll(rows[32 * i : 32 * i + 32], 32 * i, 1)
                    tile = jnp.where(lane < 32 * i, tile, moved)
                tiles[d, f, 256:288, :] = tile.astype(BF16)
        outs[d].start()
    for copy in outs:
        copy.wait()


def pack(coefficients):
    rows = coefficients.reshape(PER, DEPTH * COMP, GROUPS * SEG)
    return pl.pallas_call(
        pack_kernel,
        in_specs=[pl.BlockSpec(memory_space=pl.ANY)],
        out_specs=pl.BlockSpec(memory_space=pl.ANY),
        out_shape=jax.ShapeDtypeStruct((GROUPS, PER, 288, LANES), BF16),
        scratch_shapes=[
            pltpu.VMEM((GROUPS, PER, 288, LANES), BF16),
            pltpu.SemaphoreType.DMA((12,)),
        ],
        compiler_params=pltpu.CompilerParams(vmem_limit_bytes=60 * 1024 * 1024),
    )(rows)


def rows_of(frames, r):
    a = frames[pl.ds(r, 8, stride=STRIDE), :]
    b = frames[pl.ds(8 * STRIDE + r, 8, stride=STRIDE), :]
    return jnp.concatenate([a, b], axis=0)


def gather(ref, frames, box_ref, first, planes):
    s0, s1, _ = frames
    lane = lax.broadcasted_iota(jnp.int32, (MEMBERS, LANES), 1)
    start = jnp.broadcast_to(box_ref[:, 0:1], (MEMBERS, LANES))
    extent = jnp.broadcast_to(box_ref[:, 1:2], (MEMBERS, LANES))

    def inside(f):
        return (f >= start) & (f < start + extent)

    for q in range(planes):
        keep = inside(first + q)
        for c in range(COMP):
            for h, s in ((0, s0), (1, s1)):
                at = (q * COMP + c) * SEG + h * LANES
                tile = rows_of(s, (first + q) * COMP + c)
                ref[:, at : at + LANES] = jnp.where(keep, tile, 0.0).astype(BF16)
    return lane, inside


def gather_after(ref, sh, lane, inside, first, base):
    for j in range(2):
        planes = [first + 4 * j + i for i in range(4)]
        keep = inside(planes[0] + lane // CY)
        for c in range(COMP):
            packed = rows_of(sh, planes[0] * COMP + c)
            for i in range(1, 4):
                moved = pltpu.roll(rows_of(sh, planes[i] * COMP + c), 32 * i, 1)
                packed = jnp.where(lane < 32 * i, packed, moved)
            at = base + (j * COMP + c) * LANES
            ref[:, at : at + LANES] = jnp.where(keep, packed, 0.0).astype(BF16)


def place_kernel(odd_ref, start_ref, box_ref, in_ref, across_ref, s0, s1, sh):
    for n in range(MEMBERS):
        at = pl.multiple_of(n * STRIDE + start_ref[n] * COMP, 8)
        s0[pl.ds(at, 128), :] = in_ref[n, 0:128, :].astype(F32)
        s1[pl.ds(at, 128), :] = in_ref[n, 128:256, :].astype(F32)
        packed = in_ref[n, 256:288, :].astype(F32)
        for i in range(4):
            part = packed if i == 0 else pltpu.roll(packed, LANES - 32 * i, 1)
            sh[pl.ds(pl.multiple_of(at + 32 * i, 8), 32), :] = part
    odd = odd_ref[0]
    lane, inside = gather(across_ref, (s0, s1, sh), box_ref, odd * 15, 8)
    gather_after(across_ref, sh, lane, inside, odd * 16, MAIN)


def place(odd, starts, box, got):
    whole = pl.BlockSpec(memory_space=pltpu.VMEM)
    scalars = pl.BlockSpec(memory_space=pltpu.SMEM)
    return pl.pallas_call(
        place_kernel,
        in_specs=[scalars] * 2 + [whole] * 2,
        out_specs=[whole] * 4,
        out_shape=[jax.ShapeDtypeStruct((MEMBERS, MAIN + HALO), BF16)]
        + [jax.ShapeDtypeStruct((MEMBERS * STRIDE, LANES), F32)] * 3,
        compiler_params=params(),
    )(odd, starts, box, got.reshape(MEMBERS, 288, LANES))


def place_near_kernel(odd_ref, box_ref, _across, s0, s1, sh, chip_ref, mid_ref):
    even = 1 - odd_ref[0]
    frames = (s0, s1, sh)
    lane, inside = gather(chip_ref, frames, box_ref, even * 15, 8)
    gather_after(chip_ref, sh, lane, inside, even * 16, MAIN)
    gather(mid_ref, frames, box_ref, 7, 9)
    gather_after(mid_ref, sh, lane, inside, 8, FULL)


def place_near(odd, box, across, frames):
    whole = pl.BlockSpec(memory_space=pltpu.VMEM)
    return pl.pallas_call(
        place_near_kernel,
        in_specs=[pl.BlockSpec(memory_space=pltpu.SMEM), whole, pl.BlockSpec(memory_space=pl.ANY)] + [whole] * 3,
        out_specs=[whole] * 2,
        out_shape=[
            jax.ShapeDtypeStruct((MEMBERS, MAIN + HALO), BF16),
            jax.ShapeDtypeStruct((MEMBERS, FULL + HALO), BF16),
        ],
        compiler_params=params(),
        cost_estimate=SMALL,
    )(odd, box, across, *frames)


def signed_sums(values):
    values = list(values)
    for bit in (1, 2, 4):
        values = [
            values[k ^ bit] - values[k] if k & bit else values[k] + values[k ^ bit]
            for k in range(COMP)
        ]
    return values


def apply_planes(src, src_at, dst, dst_at, where_ref, where_at, pot_ref, lap_ref):
    rel = where_ref[where_at : where_at + 16, 0:1]
    ext = where_ref[where_at : where_at + 16, 1:2]

    def plane(q, c):
        lanes = (q + 1) * PLANE + c * SEG
        return src[src_at : src_at + 16, lanes : lanes + SEG]

    for q in range(-1, SZ):
        inside = jnp.where((q >= rel) & (q < rel + ext), -0.5, 0.0)
        if q < 0:
            totals = [inside * plane(0, c).astype(F32) for c in range(COMP)]
        else:
            here = [plane(q, c) for c in range(COMP)]
            plane_term = jnp.dot(
                jnp.concatenate(here, axis=0), lap_ref[...], preferred_element_type=F32
            )
            orbital = [v.astype(F32) for v in here]
            fine = signed_sums(orbital)
            pot = pot_ref[q * COMP : q * COMP + COMP, :]
            back = signed_sums([fine[k] * pot[k : k + 1] for k in range(COMP)])
            totals = []
            for c in range(COMP):
                beside = plane(q - 1, c).astype(F32)
                if q < SZ - 1:
                    beside += plane(q + 1, c).astype(F32)
                total = plane_term[16 * c : 16 * c + 16] + back[c]
                totals.append(total + inside * beside)
        for c in range(COMP):
            lanes = (q + 1) * PLANE + c * SEG
            dst[dst_at : dst_at + 16, lanes : lanes + SEG] = totals[c].astype(BF16)


def fill(dst, at, src_ref, above):
    blank = jnp.zeros((16, PLANE), BF16)
    dst[at : at + 16, pl.ds(pl.multiple_of(above * PLANE, LANES), MAIN)] = src_ref[:, 0:MAIN]
    dst[at : at + 16, pl.ds(pl.multiple_of((1 - above) * MAIN, LANES), PLANE)] = blank


def last_rows(dst, dst_at, src, rows):
    lane = lax.broadcasted_iota(jnp.int32, (rows, LANES), 1)
    for j in range(2):
        for c in range(COMP):
            packed = None
            for i in range(4):
                at = PLANE + ((4 * j + i) * COMP + c) * SEG + LANES
                piece = src[0:rows, at : at + LANES].astype(F32)
                if i < 3:
                    piece = pltpu.roll(piece, 32 * (i + 1), 1)
                packed = piece if packed is None else jnp.where(lane < 32 * i, packed, piece)
            at = (j * COMP + c) * LANES
            dst[dst_at : dst_at + rows, at : at + LANES] = packed.astype(BF16)


def contract(a, b):
    return lax.dot_general(a, b, (((1,), (1,)), ((), ())), preferred_element_type=F32)


def near_kernel(odd_ref, share_ref, chip_ref, mid_ref, where_ref, pot_ref, lap_ref, both_ref, last_ref, halo_ref, sum_ref):
    fill(both_ref, 0, chip_ref, 1 - odd_ref[0])
    both_ref[16:32, :] = mid_ref[:, 0:FULL]
    halo_ref[0:16, :] = chip_ref[:, MAIN : MAIN + HALO]
    halo_ref[16:32, :] = mid_ref[:, FULL : FULL + HALO]
    for at in (0, 16):
        apply_planes(both_ref, at, both_ref, 32 + at, where_ref, at, pot_ref, lap_ref)
    last_rows(last_ref, 0, both_ref, 32)
    sums = contract(both_ref[:, PLANE:FULL], both_ref[0:32, PLANE:FULL])
    sum_ref[0:32, 0:32] = sums[0:32]
    below = contract(both_ref[32:64, 0:PLANE], both_ref[0:32, 0:PLANE])
    cross = contract(last_ref[...], halo_ref[...]) + contract(halo_ref[...], last_ref[...])
    sum_ref[32:64, 0:32] = sums[32:64] + below + jnp.where(share_ref[0] > 0, -0.5, 0.0) * cross


def near(odd, share, chip, mid, where, pot, laplace):
    whole = pl.BlockSpec(memory_space=pltpu.VMEM)
    return pl.pallas_call(
        near_kernel,
        in_specs=[pl.BlockSpec(memory_space=pltpu.SMEM)] * 2 + [whole] * 5,
        out_specs=[whole] * 4,
        out_shape=[
            jax.ShapeDtypeStruct((64, FULL), BF16),
            jax.ShapeDtypeStruct((32, HALO), BF16),
            jax.ShapeDtypeStruct((32, HALO), BF16),
            jax.ShapeDtypeStruct((64, LANES), F32),
        ],
        compiler_params=params(),
        cost_estimate=SMALL,
    )(odd, share, chip, mid, where, pot, laplace)


def far_kernel(
    odd_ref, share_ref, across_ref, both_ref, last_ref, halo_ref, sum_ref, where_ref, pot_ref, lap_ref,
    out_ref, far, last, sums, turn,
):
    odd = odd_ref[0]
    fill(far, 0, across_ref, odd)
    halo = across_ref[:, MAIN : MAIN + HALO]
    last_rows(last, 0, far, 16)
    apply_planes(far, 0, far, 16, where_ref, 32, pot_ref, lap_ref)
    main, below = slice(PLANE, FULL), slice(0, PLANE)
    table = contract(jnp.concatenate([both_ref[:, main], far[:, main]], axis=0), far[:, main])
    below_table = contract(jnp.concatenate([both_ref[:, below], far[:, below]], axis=0), far[:, below])
    cols = lax.broadcasted_iota(jnp.int32, (32, 32), 1)
    factor = jnp.where(share_ref[0] > 0, -0.5, 0.0)
    cross = factor * (contract(last_ref[...], halo) + contract(halo_ref[...], last[...]))
    cross_corner = factor * (contract(last[...], halo) + contract(halo, last[...]))
    turn[...] = jnp.zeros((LANES, LANES), F32)
    turn[0:32, 0:32] = table[0:32] + jnp.where(cols >= 16, below_table[0:32], 0.0)
    turn[0:32, 16:32] = turn[0:32, 16:32] + cross
    turned = turn[...].T
    rows = (turned[0:16, 0:32], turned[16:32, 0:32])
    column = (table[0:32, 0:16], table[32:64, 0:16] + below_table[32:64, 0:16] + cross)
    corner = (table[64:80, 0:16], table[80:96, 0:16] + below_table[80:96, 0:16] + cross_corner)
    sums[...] = jnp.zeros((96, LANES), F32)
    for k in range(2):
        at = 48 * k
        sums[at : at + 32, 0:32] = sum_ref[32 * k : 32 * k + 32, 0:32]
        sums[at + 32 : at + 48, 0:32] = rows[k]
        sums[at : at + 32, 32:48] = column[k]
        sums[at + 32 : at + 48, 32:48] = corner[k]
    lane = lax.broadcasted_iota(jnp.int32, (96, LANES), 1)
    table = sums[...]
    chip_up = pltpu.roll(table, 32, 1)
    across_down = pltpu.roll(table, LANES - 32, 1)
    even = jnp.where(lane < 16, across_down, jnp.where(lane < 32, table, chip_up))
    even = jnp.where(lane < 48, even, 0.0)
    table = jnp.where(odd > 0, table, even)
    sums[0:48, :] = table[0:48] + pltpu.roll(table[48:96], 64, 1)
    for x in range(GROUPS):
        here = odd * GROUPS + x
        there = (1 - odd) * GROUPS + x
        out_ref[here, 0:PER, :] = sums[16 + PER * x : 16 + PER * x + PER, :]
        out_ref[here, PER : 2 * PER, :] = sums[32 + PER * x : 32 + PER * x + PER, :]
        out_ref[there, 0:PER, :] = sums[PER * x : PER * x + PER, :]
        out_ref[there, PER : 2 * PER, :] = jnp.zeros((PER, LANES), F32)


def far(odd, share, across, both, last, halo, sums, where, pot, laplace):
    whole = pl.BlockSpec(memory_space=pltpu.VMEM)
    scalar = pl.BlockSpec(memory_space=pltpu.SMEM)
    return pl.pallas_call(
        far_kernel,
        in_specs=[scalar, scalar] + [whole] * 8,
        out_specs=whole,
        out_shape=jax.ShapeDtypeStruct((2 * GROUPS, 2 * PER, LANES), F32),
        scratch_shapes=[
            pltpu.VMEM((32, FULL), BF16),
            pltpu.VMEM((16, HALO), BF16),
            pltpu.VMEM((96, LANES), F32),
            pltpu.VMEM((LANES, LANES), F32),
        ],
        compiler_params=params(),
    )(odd, share, across, both, last, halo, sums, where, pot, laplace)


def settle_kernel(odd_ref, parts_ref, rows_ref, far_ref):
    odd = odd_ref[0]
    here, there = odd * GROUPS, (1 - odd) * GROUPS
    same, other = parts_ref[here], parts_ref[there]
    for x in range(1, GROUPS):
        same += parts_ref[here + x]
        other += parts_ref[there + x]
    rows_ref[0:8, :] = same
    rows_ref[8:16, :] = other
    far_ref[...] = same[PER:, :]


def settle(odd, parts):
    whole = pl.BlockSpec(memory_space=pltpu.VMEM)
    return pl.pallas_call(
        settle_kernel,
        in_specs=[pl.BlockSpec(memory_space=pltpu.SMEM), whole],
        out_specs=[whole] * 2,
        out_shape=[jax.ShapeDtypeStruct((16, LANES), F32), jax.ShapeDtypeStruct((PER, LANES), F32)],
        compiler_params=pltpu.CompilerParams(vmem_limit_bytes=4 * 1024 * 1024),
    )(odd, parts)


def finish_kernel(odd_ref, rows_ref, far_ref, margin_ref, ham_ref, far):
    odd = odd_ref[0] > 0
    far[...] = jnp.zeros(far.shape, F32)
    far[0:PER, :] = far_ref[...]
    own, chip, across = rows_ref[0:8, :], rows_ref[8:16, :], far[...]
    blocks = (jnp.where(odd, chip, across), own, jnp.where(odd, across, chip))
    lane = lax.broadcasted_iota(jnp.int32, (8, LANES), 1)
    for ref, first in ((margin_ref, 0), (ham_ref, 64)):
        band = jnp.zeros((8, LANES), F32)
        for k in range(3):
            turn = (16 * k - first) % LANES
            value = blocks[k] if turn == 0 else pltpu.roll(blocks[k], turn, 1)
            band += jnp.where((lane >= 16 * k) & (lane < 16 * k + 48), value, 0.0)
        ref[...] = band[0:PER, 0:80]


def finish(odd, rows, far_rows):
    whole = pl.BlockSpec(memory_space=pltpu.VMEM)
    return pl.pallas_call(
        finish_kernel,
        in_specs=[pl.BlockSpec(memory_space=pltpu.SMEM)] + [whole] * 2,
        out_specs=[whole] * 2,
        out_shape=[jax.ShapeDtypeStruct((PER, 80), F32)] * 2,
        scratch_shapes=[pltpu.VMEM((8, LANES), F32)],
        compiler_params=pltpu.CompilerParams(vmem_limit_bytes=4 * 1024 * 1024),
    )(odd, rows, far_rows)


def segment_laplace():
    cells = jnp.arange(SEG, dtype=jnp.int32)
    x, y = cells // CY, cells % CY
    step_x = jnp.abs(x[:, None] - x[None, :])
    step_y = jnp.abs(y[:, None] - y[None, :])
    return jnp.where(
        step_x + step_y == 0, 3.0, jnp.where(step_x + step_y == 1, -0.5, 0.0)
    ).astype(BF16)


def local(potential, coefficients, box_center, box_extent):
    slab = lax.axis_index("slab")
    group = lax.axis_index("grp")
    slabs = lax.axis_size("slab")
    odd = slab % 2
    on_chip = [(s, s ^ 1) for s in range(slabs)]
    across_chips = [(s, (s + 2 * (s % 2) - 1) % slabs) for s in range(slabs)]
    chips = [
        [(2 * c + k) * GROUPS + x for k in range(2) for x in range(GROUPS)] for c in range(slabs // 2)
    ]

    def frames(step):
        source = (slab + step) % slabs
        extents = lax.dynamic_slice_in_dim(box_extent, source * MEMBERS, MEMBERS)
        centers = lax.dynamic_slice_in_dim(box_center, source * MEMBERS, MEMBERS)
        return centers - source * SZ - extents // 2 + step * SZ, extents

    around = [frames(step) for step in (1 - 2 * odd, 0, 2 * odd - 1)]
    where = jnp.stack(
        [jnp.concatenate([r for r, _ in around]), jnp.concatenate([e for _, e in around])], axis=1
    )
    starts, extents = around[1]
    pot = lax.dynamic_slice_in_dim(potential, group * SEG, SEG, axis=2)
    pot = pot.reshape(SZ * COMP, SEG).astype(F32) * (1.0 / COMP)
    laplace = segment_laplace()
    share = (group < GROUPS - 1).astype(jnp.int32).reshape(1)
    flag = odd.astype(jnp.int32).reshape(1)

    got = lax.all_to_all(pack(coefficients), "grp", 0, 0, tiled=True)
    box = jnp.stack([starts + SZ, extents], axis=1)
    across, *placed = place(flag, starts + SZ, box, got)
    chip, mid = place_near(flag, box, across, placed)
    across = lax.ppermute(across, "slab", across_chips)
    chip = lax.ppermute(chip, "slab", on_chip)
    both, last, halo, sums = near(flag, share, chip, mid, where, pot, laplace)
    parts = far(flag, share, across, both, last, halo, sums, where, pot, laplace)
    parts = lax.all_to_all(
        parts, ("slab", "grp"), 0, 0, tiled=True, axis_index_groups=chips
    )
    rows, far_rows = settle(flag, parts)
    return finish(flag, rows, lax.ppermute(far_rows, "slab", across_chips))


def solution(mesh):
    return jax.shard_map(
        local,
        mesh=mesh,
        in_specs=(P("slab", None, None), P(("slab", "grp"), None, None, None), P(), P()),
        out_specs=(P(("slab", "grp"), None), P(("slab", "grp"), None)),
        check_vma=False,
    )
```

```python
import jax
import jax.numpy as jnp
from jax import lax
from jax.experimental import pallas as pl
from jax.experimental.pallas import tpu as pltpu
from jax.sharding import PartitionSpec as P

GROUPS = 4
PER = 4
MEMBERS = 16
DEPTH = 16
SZ = 8
COMP = 8
CY = 32
SEG = 256
LANES = 128
PLANE = COMP * SEG
MAIN = SZ * PLANE
FULL = MAIN + PLANE
HALO = SZ * COMP * CY
STRIDE = 27 * COMP
VMEM = 20 * 1024 * 1024
F32 = jnp.float32
BF16 = jnp.bfloat16


SMALL = pl.CostEstimate(flops=1, bytes_accessed=1, transcendentals=0)


def params():
    return pltpu.CompilerParams(vmem_limit_bytes=VMEM)


def pack_kernel(in_ref, _start, _box, out_ref):
    lane = lax.broadcasted_iota(jnp.int32, (32, LANES), 1)
    for f in range(PER):
        for d in range(GROUPS):
            out_ref[d, f, 0:128, :] = in_ref[f, :, d * SEG : d * SEG + LANES]
            out_ref[d, f, 128:256, :] = in_ref[f, :, d * SEG + LANES : d * SEG + SEG]
            if d == GROUPS - 1:
                out_ref[d, f, 256:288, :] = jnp.zeros((32, LANES), BF16)
            else:
                after = in_ref[f, :, d * SEG + SEG : d * SEG + SEG + LANES].astype(F32)
                tile = after[0:32]
                for i in range(1, 4):
                    moved = pltpu.roll(after[32 * i : 32 * i + 32], 32 * i, 1)
                    tile = jnp.where(lane < 32 * i, tile, moved)
                out_ref[d, f, 256:288, :] = tile.astype(BF16)


def pack(coefficients, starts, box):
    rows = coefficients.reshape(PER, DEPTH * COMP, GROUPS * SEG)
    whole = pl.BlockSpec(memory_space=pltpu.VMEM)
    return pl.pallas_call(
        pack_kernel,
        in_specs=[whole] + [pl.BlockSpec(memory_space=pl.ANY)] * 2,
        out_specs=whole,
        out_shape=jax.ShapeDtypeStruct((GROUPS, PER, 288, LANES), BF16),
        compiler_params=params(),
    )(rows, starts, box)


def rows_of(frames, r):
    a = frames[pl.ds(r, 8, stride=STRIDE), :]
    b = frames[pl.ds(8 * STRIDE + r, 8, stride=STRIDE), :]
    return jnp.concatenate([a, b], axis=0)


def gather(ref, frames, box_ref, first, planes):
    s0, s1, _ = frames
    lane = lax.broadcasted_iota(jnp.int32, (MEMBERS, LANES), 1)
    start = jnp.broadcast_to(box_ref[:, 0:1], (MEMBERS, LANES))
    extent = jnp.broadcast_to(box_ref[:, 1:2], (MEMBERS, LANES))

    def inside(f):
        return (f >= start) & (f < start + extent)

    for q in range(planes):
        keep = inside(first + q)
        for c in range(COMP):
            for h, s in ((0, s0), (1, s1)):
                at = (q * COMP + c) * SEG + h * LANES
                tile = rows_of(s, (first + q) * COMP + c)
                ref[:, at : at + LANES] = jnp.where(keep, tile, 0.0).astype(BF16)
    return lane, inside


def gather_after(ref, sh, lane, inside, first, base):
    for j in range(2):
        planes = [first + 4 * j + i for i in range(4)]
        keep = inside(planes[0] + lane // CY)
        for c in range(COMP):
            packed = rows_of(sh, planes[0] * COMP + c)
            for i in range(1, 4):
                moved = pltpu.roll(rows_of(sh, planes[i] * COMP + c), 32 * i, 1)
                packed = jnp.where(lane < 32 * i, packed, moved)
            at = base + (j * COMP + c) * LANES
            ref[:, at : at + LANES] = jnp.where(keep, packed, 0.0).astype(BF16)


def place_kernel(odd_ref, start_ref, box_ref, in_ref, across_ref, s0, s1, sh):
    for n in range(MEMBERS):
        at = pl.multiple_of(n * STRIDE + start_ref[n] * COMP, 8)
        s0[pl.ds(at, 128), :] = in_ref[n, 0:128, :].astype(F32)
        s1[pl.ds(at, 128), :] = in_ref[n, 128:256, :].astype(F32)
        packed = in_ref[n, 256:288, :].astype(F32)
        for i in range(4):
            part = packed if i == 0 else pltpu.roll(packed, LANES - 32 * i, 1)
            sh[pl.ds(pl.multiple_of(at + 32 * i, 8), 32), :] = part
    odd = odd_ref[0]
    lane, inside = gather(across_ref, (s0, s1, sh), box_ref, odd * 15, 8)
    gather_after(across_ref, sh, lane, inside, odd * 16, MAIN)


def place(odd, starts, box, got):
    whole = pl.BlockSpec(memory_space=pltpu.VMEM)
    scalars = pl.BlockSpec(memory_space=pltpu.SMEM)
    return pl.pallas_call(
        place_kernel,
        in_specs=[scalars] * 2 + [whole] * 2,
        out_specs=[whole] * 4,
        out_shape=[jax.ShapeDtypeStruct((MEMBERS, MAIN + HALO), BF16)]
        + [jax.ShapeDtypeStruct((MEMBERS * STRIDE, LANES), F32)] * 3,
        compiler_params=params(),
    )(odd, starts, box, got.reshape(MEMBERS, 288, LANES))


def place_near_kernel(odd_ref, box_ref, _across, s0, s1, sh, chip_ref, mid_ref):
    even = 1 - odd_ref[0]
    frames = (s0, s1, sh)
    lane, inside = gather(chip_ref, frames, box_ref, even * 15, 8)
    gather_after(chip_ref, sh, lane, inside, even * 16, MAIN)
    gather(mid_ref, frames, box_ref, 7, 9)
    gather_after(mid_ref, sh, lane, inside, 8, FULL)


def place_near(odd, box, across, frames):
    whole = pl.BlockSpec(memory_space=pltpu.VMEM)
    return pl.pallas_call(
        place_near_kernel,
        in_specs=[pl.BlockSpec(memory_space=pltpu.SMEM), whole, pl.BlockSpec(memory_space=pl.ANY)] + [whole] * 3,
        out_specs=[whole] * 2,
        out_shape=[
            jax.ShapeDtypeStruct((MEMBERS, MAIN + HALO), BF16),
            jax.ShapeDtypeStruct((MEMBERS, FULL + HALO), BF16),
        ],
        compiler_params=params(),
        cost_estimate=SMALL,
    )(odd, box, across, *frames)


def signed_sums(values):
    values = list(values)
    for bit in (1, 2, 4):
        values = [
            values[k ^ bit] - values[k] if k & bit else values[k] + values[k ^ bit]
            for k in range(COMP)
        ]
    return values


def apply_planes(src, src_at, dst, dst_at, where_ref, where_at, pot_ref, lap_ref):
    rel = where_ref[where_at : where_at + 16, 0:1]
    ext = where_ref[where_at : where_at + 16, 1:2]

    def plane(q, c):
        lanes = (q + 1) * PLANE + c * SEG
        return src[src_at : src_at + 16, lanes : lanes + SEG]

    for q in range(-1, SZ):
        inside = jnp.where((q >= rel) & (q < rel + ext), -0.5, 0.0)
        if q < 0:
            totals = [inside * plane(0, c).astype(F32) for c in range(COMP)]
        else:
            here = [plane(q, c) for c in range(COMP)]
            plane_term = jnp.dot(
                jnp.concatenate(here, axis=0), lap_ref[...], preferred_element_type=F32
            )
            orbital = [v.astype(F32) for v in here]
            fine = signed_sums(orbital)
            pot = pot_ref[q * COMP : q * COMP + COMP, :]
            back = signed_sums([fine[k] * pot[k : k + 1] for k in range(COMP)])
            totals = []
            for c in range(COMP):
                beside = plane(q - 1, c).astype(F32)
                if q < SZ - 1:
                    beside += plane(q + 1, c).astype(F32)
                total = plane_term[16 * c : 16 * c + 16] + back[c]
                totals.append(total + inside * beside)
        for c in range(COMP):
            lanes = (q + 1) * PLANE + c * SEG
            dst[dst_at : dst_at + 16, lanes : lanes + SEG] = totals[c].astype(BF16)


def fill(dst, at, src_ref, above):
    blank = jnp.zeros((16, PLANE), BF16)
    dst[at : at + 16, pl.ds(pl.multiple_of(above * PLANE, LANES), MAIN)] = src_ref[:, 0:MAIN]
    dst[at : at + 16, pl.ds(pl.multiple_of((1 - above) * MAIN, LANES), PLANE)] = blank


def last_rows(dst, dst_at, src, rows):
    lane = lax.broadcasted_iota(jnp.int32, (rows, LANES), 1)
    for j in range(2):
        for c in range(COMP):
            packed = None
            for i in range(4):
                at = PLANE + ((4 * j + i) * COMP + c) * SEG + LANES
                piece = src[0:rows, at : at + LANES].astype(F32)
                if i < 3:
                    piece = pltpu.roll(piece, 32 * (i + 1), 1)
                packed = piece if packed is None else jnp.where(lane < 32 * i, packed, piece)
            at = (j * COMP + c) * LANES
            dst[dst_at : dst_at + rows, at : at + LANES] = packed.astype(BF16)


def contract(a, b):
    return lax.dot_general(a, b, (((1,), (1,)), ((), ())), preferred_element_type=F32)


def near_kernel(odd_ref, share_ref, chip_ref, mid_ref, where_ref, pot_ref, lap_ref, both_ref, last_ref, halo_ref, sum_ref):
    fill(both_ref, 0, chip_ref, 1 - odd_ref[0])
    both_ref[16:32, :] = mid_ref[:, 0:FULL]
    halo_ref[0:16, :] = chip_ref[:, MAIN : MAIN + HALO]
    halo_ref[16:32, :] = mid_ref[:, FULL : FULL + HALO]
    for at in (0, 16):
        apply_planes(both_ref, at, both_ref, 32 + at, where_ref, at, pot_ref, lap_ref)
    last_rows(last_ref, 0, both_ref, 32)
    sums = contract(both_ref[:, PLANE:FULL], both_ref[0:32, PLANE:FULL])
    sum_ref[0:32, 0:32] = sums[0:32]
    below = contract(both_ref[32:64, 0:PLANE], both_ref[0:32, 0:PLANE])
    cross = contract(last_ref[...], halo_ref[...]) + contract(halo_ref[...], last_ref[...])
    sum_ref[32:64, 0:32] = sums[32:64] + below + jnp.where(share_ref[0] > 0, -0.5, 0.0) * cross


def near(odd, share, chip, mid, where, pot, laplace):
    whole = pl.BlockSpec(memory_space=pltpu.VMEM)
    return pl.pallas_call(
        near_kernel,
        in_specs=[pl.BlockSpec(memory_space=pltpu.SMEM)] * 2 + [whole] * 5,
        out_specs=[whole] * 4,
        out_shape=[
            jax.ShapeDtypeStruct((64, FULL), BF16),
            jax.ShapeDtypeStruct((32, HALO), BF16),
            jax.ShapeDtypeStruct((32, HALO), BF16),
            jax.ShapeDtypeStruct((64, LANES), F32),
        ],
        compiler_params=params(),
        cost_estimate=SMALL,
    )(odd, share, chip, mid, where, pot, laplace)


def far_kernel(
    odd_ref, share_ref, across_ref, both_ref, last_ref, halo_ref, sum_ref, where_ref, pot_ref, lap_ref,
    out_ref, far, last, sums, turn,
):
    odd = odd_ref[0]
    fill(far, 0, across_ref, odd)
    halo = across_ref[:, MAIN : MAIN + HALO]
    last_rows(last, 0, far, 16)
    apply_planes(far, 0, far, 16, where_ref, 32, pot_ref, lap_ref)
    main, below = slice(PLANE, FULL), slice(0, PLANE)
    table = contract(jnp.concatenate([both_ref[:, main], far[:, main]], axis=0), far[:, main])
    below_table = contract(jnp.concatenate([both_ref[:, below], far[:, below]], axis=0), far[:, below])
    cols = lax.broadcasted_iota(jnp.int32, (32, 32), 1)
    factor = jnp.where(share_ref[0] > 0, -0.5, 0.0)
    cross = factor * (contract(last_ref[...], halo) + contract(halo_ref[...], last[...]))
    cross_corner = factor * (contract(last[...], halo) + contract(halo, last[...]))
    turn[...] = jnp.zeros((LANES, LANES), F32)
    turn[0:32, 0:32] = table[0:32] + jnp.where(cols >= 16, below_table[0:32], 0.0)
    turn[0:32, 16:32] = turn[0:32, 16:32] + cross
    turned = turn[...].T
    rows = (turned[0:16, 0:32], turned[16:32, 0:32])
    column = (table[0:32, 0:16], table[32:64, 0:16] + below_table[32:64, 0:16] + cross)
    corner = (table[64:80, 0:16], table[80:96, 0:16] + below_table[80:96, 0:16] + cross_corner)
    sums[...] = jnp.zeros((96, LANES), F32)
    for k in range(2):
        at = 48 * k
        sums[at : at + 32, 0:32] = sum_ref[32 * k : 32 * k + 32, 0:32]
        sums[at + 32 : at + 48, 0:32] = rows[k]
        sums[at : at + 32, 32:48] = column[k]
        sums[at + 32 : at + 48, 32:48] = corner[k]
    lane = lax.broadcasted_iota(jnp.int32, (96, LANES), 1)
    table = sums[...]
    chip_up = pltpu.roll(table, 32, 1)
    across_down = pltpu.roll(table, LANES - 32, 1)
    even = jnp.where(lane < 16, across_down, jnp.where(lane < 32, table, chip_up))
    even = jnp.where(lane < 48, even, 0.0)
    table = jnp.where(odd > 0, table, even)
    sums[0:48, :] = table[0:48] + pltpu.roll(table[48:96], 64, 1)
    for x in range(GROUPS):
        here = odd * GROUPS + x
        there = (1 - odd) * GROUPS + x
        out_ref[here, 0:PER, :] = sums[16 + PER * x : 16 + PER * x + PER, :]
        out_ref[here, PER : 2 * PER, :] = sums[32 + PER * x : 32 + PER * x + PER, :]
        out_ref[there, 0:PER, :] = sums[PER * x : PER * x + PER, :]
        out_ref[there, PER : 2 * PER, :] = jnp.zeros((PER, LANES), F32)


def far(odd, share, across, both, last, halo, sums, where, pot, laplace):
    whole = pl.BlockSpec(memory_space=pltpu.VMEM)
    scalar = pl.BlockSpec(memory_space=pltpu.SMEM)
    return pl.pallas_call(
        far_kernel,
        in_specs=[scalar, scalar] + [whole] * 8,
        out_specs=whole,
        out_shape=jax.ShapeDtypeStruct((2 * GROUPS, 2 * PER, LANES), F32),
        scratch_shapes=[
            pltpu.VMEM((32, FULL), BF16),
            pltpu.VMEM((16, HALO), BF16),
            pltpu.VMEM((96, LANES), F32),
            pltpu.VMEM((LANES, LANES), F32),
        ],
        compiler_params=params(),
    )(odd, share, across, both, last, halo, sums, where, pot, laplace)


def settle_kernel(odd_ref, parts_ref, rows_ref, far_ref):
    odd = odd_ref[0]
    here, there = odd * GROUPS, (1 - odd) * GROUPS
    same, other = parts_ref[here], parts_ref[there]
    for x in range(1, GROUPS):
        same += parts_ref[here + x]
        other += parts_ref[there + x]
    rows_ref[0:8, :] = same
    rows_ref[8:16, :] = other
    far_ref[...] = same[PER:, :]


def settle(odd, parts):
    whole = pl.BlockSpec(memory_space=pltpu.VMEM)
    return pl.pallas_call(
        settle_kernel,
        in_specs=[pl.BlockSpec(memory_space=pltpu.SMEM), whole],
        out_specs=[whole] * 2,
        out_shape=[jax.ShapeDtypeStruct((16, LANES), F32), jax.ShapeDtypeStruct((PER, LANES), F32)],
        compiler_params=pltpu.CompilerParams(vmem_limit_bytes=4 * 1024 * 1024),
    )(odd, parts)


def finish_kernel(odd_ref, rows_ref, far_ref, margin_ref, ham_ref, far):
    odd = odd_ref[0] > 0
    far[...] = jnp.zeros(far.shape, F32)
    far[0:PER, :] = far_ref[...]
    own, chip, across = rows_ref[0:8, :], rows_ref[8:16, :], far[...]
    blocks = (jnp.where(odd, chip, across), own, jnp.where(odd, across, chip))
    lane = lax.broadcasted_iota(jnp.int32, (8, LANES), 1)
    for ref, first in ((margin_ref, 0), (ham_ref, 64)):
        band = jnp.zeros((8, LANES), F32)
        for k in range(3):
            turn = (16 * k - first) % LANES
            value = blocks[k] if turn == 0 else pltpu.roll(blocks[k], turn, 1)
            band += jnp.where((lane >= 16 * k) & (lane < 16 * k + 48), value, 0.0)
        ref[...] = band[0:PER, 0:80]


def finish(odd, rows, far_rows):
    whole = pl.BlockSpec(memory_space=pltpu.VMEM)
    return pl.pallas_call(
        finish_kernel,
        in_specs=[pl.BlockSpec(memory_space=pltpu.SMEM)] + [whole] * 2,
        out_specs=[whole] * 2,
        out_shape=[jax.ShapeDtypeStruct((PER, 80), F32)] * 2,
        scratch_shapes=[pltpu.VMEM((8, LANES), F32)],
        compiler_params=pltpu.CompilerParams(vmem_limit_bytes=4 * 1024 * 1024),
    )(odd, rows, far_rows)


def segment_laplace():
    cells = jnp.arange(SEG, dtype=jnp.int32)
    x, y = cells // CY, cells % CY
    step_x = jnp.abs(x[:, None] - x[None, :])
    step_y = jnp.abs(y[:, None] - y[None, :])
    return jnp.where(
        step_x + step_y == 0, 3.0, jnp.where(step_x + step_y == 1, -0.5, 0.0)
    ).astype(BF16)


def local(potential, coefficients, box_center, box_extent):
    slab = lax.axis_index("slab")
    group = lax.axis_index("grp")
    slabs = lax.axis_size("slab")
    odd = slab % 2
    on_chip = [(s, s ^ 1) for s in range(slabs)]
    across_chips = [(s, (s + 2 * (s % 2) - 1) % slabs) for s in range(slabs)]
    chips = [
        [(2 * c + k) * GROUPS + x for k in range(2) for x in range(GROUPS)] for c in range(slabs // 2)
    ]

    def frames(step):
        source = (slab + step) % slabs
        extents = lax.dynamic_slice_in_dim(box_extent, source * MEMBERS, MEMBERS)
        centers = lax.dynamic_slice_in_dim(box_center, source * MEMBERS, MEMBERS)
        return centers - source * SZ - extents // 2 + step * SZ, extents

    around = [frames(step) for step in (1 - 2 * odd, 0, 2 * odd - 1)]
    where = jnp.stack(
        [jnp.concatenate([r for r, _ in around]), jnp.concatenate([e for _, e in around])], axis=1
    )
    starts, extents = around[1]
    pot = lax.dynamic_slice_in_dim(potential, group * SEG, SEG, axis=2)
    pot = pot.reshape(SZ * COMP, SEG).astype(F32) * (1.0 / COMP)
    laplace = segment_laplace()
    share = (group < GROUPS - 1).astype(jnp.int32).reshape(1)
    flag = odd.astype(jnp.int32).reshape(1)

    box = jnp.stack([starts + SZ, extents], axis=1)
    got = lax.all_to_all(pack(coefficients, starts + SZ, box), "grp", 0, 0, tiled=True)
    across, *placed = place(flag, starts + SZ, box, got)
    chip, mid = place_near(flag, box, across, placed)
    across = lax.ppermute(across, "slab", across_chips)
    chip = lax.ppermute(chip, "slab", on_chip)
    both, last, halo, sums = near(flag, share, chip, mid, where, pot, laplace)
    parts = far(flag, share, across, both, last, halo, sums, where, pot, laplace)
    parts = lax.all_to_all(
        parts, ("slab", "grp"), 0, 0, tiled=True, axis_index_groups=chips
    )
    rows, far_rows = settle(flag, parts)
    return finish(flag, rows, lax.ppermute(far_rows, "slab", across_chips))


def solution(mesh):
    return jax.shard_map(
        local,
        mesh=mesh,
        in_specs=(P("slab", None, None), P(("slab", "grp"), None, None, None), P(), P()),
        out_specs=(P(("slab", "grp"), None), P(("slab", "grp"), None)),
        check_vma=False,
    )
```
